128 devices in a mesh: inst: 16 (over y_lo, z, core), tp: 8 (over y_hi, x).
Axes of the slice: x: 4, y: 4 (y_hi: 2, y_lo: 2; y = y_hi * 2 + y_lo), z: 4, core: 2. Of those that a mesh axis runs over, the one named last changes fastest.
Arguments:
- hidden_rows: bfloat16 [8192, 8192], P('inst', 'tp'), may hold values from -48 to 48
- lengths: int32 [16, 4], P('inst'), may hold values from 1 to 256, 512 in all within a row
- attn_gain: float32 [8192], replicated, may hold values from 0.5 to 2
- w_joined: bfloat16 [16, 8192, 6144], P('inst', None, 'tp'), may hold values from -3 to 3, as said below
- w_out: bfloat16 [4096, 8192], P('tp'), may hold values from -0.75 to 0.75
Outputs:
- attention_out: bfloat16 [8192, 8192], P('inst', 'tp')
The draws below stay inside these ranges and needn't reach their ends.
Inputs may be any that keep to these rules, and one draw needn't show every extreme that they name: `w_joined`: only index 0, the live instance, holds the layer that the steps use.
All inputs are finite; a program needn't handle non-finite values.
Results may differ from the reference program's by a relative error of at most 0.015.
Values may be sent and summed in bfloat16 or wider, within the bound.
A program may use at most 192 MiB of HBM per device.

```python
import math
import jax
import jax.numpy as jnp
import numpy as np
from jax import lax

D = 8192
KVHEADS = 8
HD = 128
QHEADS = 32
ROWS = 512
PROMPTS = 4
LONGEST = 256
QW = 4096
KVW = 1024
JOINED = 6144
N_INST = 16
N_TP = 8


def draw_hidden_rows(key, part):
    key = jax.random.fold_in(key, 3)
    first_key = jax.random.fold_in(key, 0)
    row_total = ROWS * N_INST
    column = jnp.arange(D, dtype=jnp.float32)
    spread = 0.3 * jnp.exp(math.log(10.0) * column / (D - 1))
    values = jnp.clip(jax.random.normal(first_key, (row_total, D), jnp.float32), -4.0, 4.0) * spread[None, :]
    return values.astype(jnp.bfloat16)


def draw_w_joined(key, part):
    key = jax.random.fold_in(key, 5)
    query_cols = QW // N_TP
    key_cols = KVW // N_TP
    base_values = jnp.clip(jax.random.normal(key, (N_INST, D, N_TP, query_cols + 2 * key_cols), jnp.float32), -4.0, 4.0) / math.sqrt(D)
    return base_values.reshape(N_INST, D, QW + 2 * KVW).astype(jnp.bfloat16)


def raised(values, rng, source, target, blocks, factor):
    owner, partner = [(jnp.arange(values.shape[dim]) // (values.shape[dim] // blocks)).reshape([-1 if axis == dim else 1 for axis in range(values.ndim)]) for dim in (source, target)]
    chosen = jax.random.permutation(rng, blocks)[partner]
    strong = (owner == chosen) | (owner == (partner + blocks // 2) % blocks)
    return jnp.where(strong, factor * values, values)


def block_scale(own_key, dims, shards, least, high):
    level = 1.0
    for axis_at, parts in shards:
        heights = jax.random.uniform(jax.random.fold_in(jax.random.fold_in(own_key, 6), axis_at), (parts,), jnp.float32, least / len(shards), high / len(shards))
        level = level * jnp.repeat(jnp.exp(heights), dims[axis_at] // parts).reshape((-1,) + (1,) * (len(dims) - 1 - axis_at))
    return level


def profile(number_of, total, limit, lean):
    portions = [(1 << 20) // math.isqrt(grade ** lean) + 1 for grade in range(2, number_of + 1)]
    surplus, given = total - limit - (number_of - 1), [1] * (number_of - 1)
    while surplus > 0:
        movable = [i for i in range(number_of - 1) if given[i] < limit]
        mass, left = sum([portions[i] for i in movable]), surplus
        for i in movable:
            more = min(limit - given[i], max(1, left * portions[i] // mass), surplus)
            given[i] = given[i] + more
            surplus = surplus - more
    return np.array([limit] + given)


def ragged_sizes(rng, number_of, total, most, skew):
    if number_of == 2:
        one = jax.random.randint(rng, (), max(1, total - most), min(most, total - 1) + 1)
        return jnp.stack([one, total - one])
    sizes = jnp.asarray(profile(number_of, total, most, skew), jnp.int32)
    couples = (number_of - 1) // 2
    source_of, taker = sizes[1:1 + 2 * couples:2], sizes[2:2 + 2 * couples:2]
    slack = jnp.minimum(source_of - 1, most - taker)
    shifted = jax.random.randint(jax.random.fold_in(rng, 1), (couples,), 0, 1 << 20) % (slack + 1)
    sizes = sizes.at[1:1 + 2 * couples:2].set(source_of - shifted).at[2:2 + 2 * couples:2].set(taker + shifted)
    return sizes[jax.random.permutation(jax.random.fold_in(rng, 2), number_of)]


def bell_draw_with(key, dims, scale, reach, shards, heavy, kind=jnp.bfloat16):
    values = scale * jax.random.normal(key, dims, jnp.float32)
    if shards:
        values = values * block_scale(key, dims, shards, -0.22, 0.18)
    return jnp.clip(raised(values, jax.random.fold_in(key, 3), *heavy), -reach, reach).astype(kind)


def setup_inputs(seed: int = 0) -> dict:
    arg_keys = jax.random.split(jax.random.key(seed), 6)
    hidden_rows = draw_hidden_rows(jax.random.fold_in(arg_keys[5], 71), 0)
    lengths = jax.vmap(lambda own: ragged_sizes(own, PROMPTS, ROWS, LONGEST, 2))(jax.random.split(arg_keys[1], N_INST)).reshape((N_INST, PROMPTS)).astype(jnp.int32)
    attn_gain = jnp.clip(jax.random.uniform(arg_keys[2], (D,), jnp.float32, 0.5, 2.0), 0.5, 2.0)
    w_joined = draw_w_joined(jax.random.fold_in(arg_keys[5], 71), 0)
    w_out = bell_draw_with(arg_keys[4], (QW, D), HD ** -0.5, 0.75, ((0, 8),), (0, 1, 8, 2.0))
    return {"hidden_rows": hidden_rows, "lengths": lengths, "attn_gain": attn_gain, "w_joined": w_joined, "w_out": w_out}


EPSILON = 1e-05
ROPE_BASE = 500000.0
ROPE_FACTOR = 8.0
LOW_FACTOR = 1.0
HIGH_FACTOR = 4.0
OLD_CONTEXT = 8192.0

def rope_frequencies(head_size):
    indices = jnp.arange(head_size // 2, dtype=jnp.float32)
    base_freq = jnp.exp(indices * (-2.0 * math.log(ROPE_BASE) / head_size))
    wavelength = 2.0 * math.pi / base_freq
    blending = (OLD_CONTEXT / wavelength - LOW_FACTOR) / (HIGH_FACTOR - LOW_FACTOR)
    blended = (1.0 - blending) * base_freq / ROPE_FACTOR + blending * base_freq
    slowed = jnp.where(wavelength > OLD_CONTEXT / LOW_FACTOR, base_freq / ROPE_FACTOR, blended)
    return jnp.where(wavelength < OLD_CONTEXT / HIGH_FACTOR, base_freq, slowed)

def prompt_layout(counts, row_count):
    counts = counts.astype(jnp.int32)
    prompt_ends = jnp.cumsum(counts).astype(jnp.int32)
    prompt_starts = prompt_ends - counts
    row_index = jnp.arange(row_count, dtype=jnp.int32)
    segment = lax.optimization_barrier(jnp.sum((row_index[:, None] >= prompt_ends[None, :]).astype(jnp.int32), axis=1)).astype(jnp.int32)
    prompt_index = jnp.arange(counts.shape[0], dtype=jnp.int32)
    begins = lax.optimization_barrier(jnp.sum(jnp.where(prompt_index[None, :] == segment[:, None], prompt_starts[None, :], 0), axis=1)).astype(jnp.int32)
    return (segment, row_index - begins)

def rotate(values, cosine, sine_table):
    half_size = values.shape[-1] // 2
    first_half = values[..., :half_size]
    second_half = values[..., half_size:]
    return jnp.concatenate([first_half * cosine - second_half * sine_table, second_half * cosine + first_half * sine_table], axis=-1)

def widened(array):
    return lax.optimization_barrier(array).astype(jnp.float32)

def one_instance(rows_here, counts, attn_gain, joined_weight, w_out):
    row_count = rows_here.shape[0]
    rows_wide = rows_here.astype(jnp.float32)
    inverse = lax.rsqrt(lax.optimization_barrier(jnp.mean(rows_wide * rows_wide, axis=1, keepdims=True)) + EPSILON)
    scaled = (rows_wide * attn_gain[None, :]).astype(jnp.bfloat16)
    projection = jnp.dot(scaled, joined_weight, preferred_element_type=jnp.float32) * inverse
    blocked = projection.reshape(row_count, N_TP, JOINED // N_TP)
    query_cols = QW // N_TP
    key_cols = KVW // N_TP
    query_heads = blocked[:, :, :query_cols].reshape(row_count, QHEADS, HD)
    key_heads = blocked[:, :, query_cols:query_cols + key_cols].reshape(row_count, KVHEADS, HD)
    value_heads = blocked[:, :, query_cols + key_cols:].reshape(row_count, KVHEADS, HD).astype(jnp.bfloat16)
    segment, position = prompt_layout(counts, row_count)
    angles = position.astype(jnp.float32)[:, None] * rope_frequencies(HD)[None, :]
    cosine = jnp.cos(angles)[:, None, :]
    sine_table = jnp.sin(angles)[:, None, :]
    query_heads = rotate(query_heads, cosine, sine_table).astype(jnp.bfloat16)
    key_heads = rotate(key_heads, cosine, sine_table).astype(jnp.bfloat16)
    group_size = QHEADS // KVHEADS
    grouped = query_heads.reshape(row_count, KVHEADS, group_size, HD)
    scores = jnp.einsum('qkgd,skd->kgqs', widened(grouped), widened(key_heads)) * (1.0 / math.sqrt(HD))
    row_index = jnp.arange(row_count, dtype=jnp.int32)
    allowed = (segment[:, None] == segment[None, :]) & (row_index[None, :] <= row_index[:, None])
    largest = lax.optimization_barrier(jnp.max(jnp.where(allowed, scores, -1e+30), axis=3, keepdims=True))
    weights = jnp.exp(jnp.where(allowed, scores - largest, -1e+30))
    denominator = lax.optimization_barrier(jnp.sum(weights, axis=3))
    rounded_weights = weights.astype(jnp.bfloat16)
    mixed = jnp.einsum('kgqs,skd->kgqd', widened(rounded_weights), widened(value_heads))
    attended = mixed / denominator[..., None]
    attended = jnp.transpose(attended, (2, 0, 1, 3)).reshape(row_count, QW).astype(jnp.bfloat16)
    column_blocks = attended.reshape(row_count, N_TP, QW // N_TP)
    out_blocks = w_out.reshape(N_TP, QW // N_TP, D)
    summed = jnp.zeros((row_count, D), jnp.float32)
    for shard_index in range(N_TP):
        partial_term = jnp.dot(column_blocks[:, shard_index, :], out_blocks[shard_index], preferred_element_type=jnp.float32).astype(jnp.bfloat16)
        summed = summed + widened(partial_term)
    return summed.astype(jnp.bfloat16)

def reference(hidden_rows, lengths, attn_gain, w_joined, w_out):
    grouped_rows = hidden_rows.reshape(N_INST, ROWS, D)
    joined_weight = w_joined[0]
    results = lax.map(lambda pair_item: one_instance(pair_item[0], pair_item[1], attn_gain, joined_weight, w_out), (grouped_rows, lengths))
    return results.reshape(N_INST * ROWS, D)
```

```python
import functools
import math

import jax
import jax.numpy as jnp
from jax import lax
from jax.experimental import pallas as pl
from jax.experimental.pallas import tpu as pltpu
from jax.sharding import PartitionSpec as P

MESH = pl.DeviceIdType.MESH
F32 = jnp.float32
BF16 = jnp.bfloat16

KVHEADS = 8
HD = 128
QHEADS = 32
ROWS = 512
D = 8192
N_TP = 8
FEATS = D // N_TP
COLS = 768
HEADS = QHEADS // N_TP
ATT_COLS = HEADS * HD
LONGEST = 256

EPSILON = 1e-05
ROPE_BASE = 500000.0
ROPE_FACTOR = 8.0
LOW_FACTOR = 1.0
HIGH_FACTOR = 4.0
OLD_CONTEXT = 8192.0

CHUNK = 32
TREE_STEPS = (43, 43, 42)
TREE_BASE = (0, 2752, 5504)
GRAY = (0, 1, 3, 2)
LAG = 4
N_SLOTS = max(TREE_STEPS) + 4 * LAG

PIECE = 128
N_PIECES = ROWS // PIECE
TQ = 128
N_Q = ROWS // TQ


def tree_masks():
    masks = [[0] * 3 for _ in range(3)]
    depths = [0] * 3
    node_of = {}
    for y_lo in range(2):
        for z in range(4):
            node_of[y_lo * 4 + GRAY[z]] = y_lo * 4 + z
    first_edges = [(0, 0), (1, 1), (1, 2), (3, 2), (3, 0), (5, 0), (7, 0)]
    for tree in range(3):
        depth = {0: 0}
        for code, dim in first_edges:
            depth[code ^ (1 << dim)] = depth[code] + 1
            turned = ((code << tree) | (code >> (3 - tree))) & 7
            masks[tree][(dim + tree) % 3] |= 1 << node_of[turned]
        for code, far in depth.items():
            turned = ((code << tree) | (code >> (3 - tree))) & 7
            depths[tree] |= far << (3 * node_of[turned])
    return masks, depths


MASKS, DEPTHS = tree_masks()


def rope_tables(start_of, rows):
    lane = lax.broadcasted_iota(jnp.int32, (1, HD), 1)
    index = lax.rem(lane, HD // 2).astype(F32)
    base = jnp.exp(index * (-2.0 * math.log(ROPE_BASE) / HD))
    wavelength = 2.0 * math.pi / base
    blending = (OLD_CONTEXT / wavelength - LOW_FACTOR) / (HIGH_FACTOR - LOW_FACTOR)
    blended = (1.0 - blending) * base / ROPE_FACTOR + blending * base
    slowed = jnp.where(wavelength > OLD_CONTEXT / LOW_FACTOR, base / ROPE_FACTOR, blended)
    frequency = jnp.where(wavelength < OLD_CONTEXT / HIGH_FACTOR, base, slowed)
    row = lax.broadcasted_iota(jnp.int32, (rows, HD), 0)
    angles = (row - start_of(row)).astype(F32) * frequency
    sine = jnp.sin(angles)
    return jnp.cos(angles), jnp.where(lane < HD // 2, -sine, sine)


def body(
    hidden, lengths, gain, w_in, wo_in, out,
    w, xs, wo, acc, att, pf, rb, own, sums, inv, cosine, sine, qb, kb, vb,
    recv_w, send_w, send_sib, recv_x, send_x, recv_s, send_s,
    recv_wx, send_wx, recv_wz, send_wz, recv_ws, send_ws, loc_wo,
    recv_a, send_a, recv_y, send_y,
):
    inst = lax.axis_index("inst")
    tp = lax.axis_index("tp")
    core = lax.rem(inst, 2)
    z = lax.rem(inst // 2, 4)
    y_lo = inst // 8
    x = lax.rem(tp, 4)
    y_hi = tp // 4

    def inst_of(y_lo_, z_, core_):
        return (y_lo_ * 4 + z_) * 2 + core_

    right = (inst, y_hi * 4 + lax.rem(x + 1, 4))
    left = (inst, y_hi * 4 + lax.rem(x + 3, 4))
    across = (inst, y_hi * 4 + lax.rem(x + 2, 4))
    opposite = (inst, (1 - y_hi) * 4 + x)
    sibling = (inst_of(y_lo, z, 1 - core), tp)
    dims = (
        (inst_of(y_lo, z + 1 - 2 * lax.rem(z, 2), core), tp),
        (inst_of(y_lo, 3 - z, core), tp),
        (inst_of(1 - y_lo, z, core), tp),
    )
    z_others = [(inst_of(y_lo, lax.rem(z + k, 4), core), tp) for k in (1, 2, 3)]
    node = y_lo * 4 + z
    source_chip = node == 0
    is_source = jnp.logical_and(source_chip, core == 0)

    def send(src, dst, s_sem, r_sem, to):
        return pltpu.make_async_remote_copy(
            src_ref=src, dst_ref=dst, send_sem=s_sem, recv_sem=r_sem, device_id=to, device_id_type=MESH
        )

    def chunk(tree, step, parity):
        at = TREE_BASE[tree] + (2 * step + parity) * CHUNK
        return pl.ds(pl.multiple_of(at, CHUNK), CHUNK)

    barrier = pltpu.get_barrier_semaphore()
    peers = [(inst, lax.rem(tp + k, N_TP)) for k in range(1, N_TP)]
    greeted = peers + z_others + [sibling, dims[2]]
    for other in greeted:
        pl.semaphore_signal(barrier, inc=1, device_id=other, device_id_type=MESH)

    @pl.when(is_source)
    def _():
        for tree in range(3):

            def load(step, carry, tree=tree):
                for parity in range(2):
                    rows = chunk(tree, step, parity)
                    pltpu.make_async_copy(
                        w_in.at[0, rows], w.at[rows], recv_w.at[tree, step, parity]
                    ).start()
                return carry

            lax.fori_loop(0, TREE_STEPS[tree], load, 0)

    foreign_cols = pl.ds(pl.multiple_of(((1 - y_hi) * 4 + x) * FEATS, FEATS), FEATS)
    own_cols = pl.ds(pl.multiple_of(tp * FEATS, FEATS), FEATS)
    wo_local = (
        pltpu.make_async_copy(wo_in.at[:, foreign_cols], wo.at[0, :, pl.ds(0, FEATS)], loc_wo.at[0]),
        pltpu.make_async_copy(wo_in.at[:, own_cols], wo.at[0, :, pl.ds(FEATS, FEATS)], loc_wo.at[1]),
    )
    for copy in wo_local:
        copy.start()

    eye = (
        lax.broadcasted_iota(jnp.int32, (128, 128), 0) == lax.broadcasted_iota(jnp.int32, (128, 128), 1)
    ).astype(F32)
    sums[tp] = jnp.zeros((8, 128), F32)
    for g in range(4):
        wide = hidden[pl.ds(g * 128, 128), :].astype(F32)
        xs[0, pl.ds(g * 128, 128), :] = (wide * gain[...]).astype(BF16)
        column = jnp.sum(wide * wide, axis=1, keepdims=True)
        sums[tp, pl.ds(g, 1), :] = jnp.sum(column * eye, axis=0, keepdims=True)

    pl.semaphore_wait(barrier, len(greeted))

    def piece(slot, p):
        return xs.at[slot, pl.ds(p * PIECE, PIECE)]

    def send_piece(src_slot, dst_slot, p, sem, to):
        send(piece(src_slot, p), piece(dst_slot, p), send_x.at[sem], recv_x.at[dst_slot, p], to).start()

    def wait_piece(slot, p):
        pltpu.make_async_copy(piece(slot, p), piece(slot, p), recv_x.at[slot, p]).wait()

    for p in range(N_PIECES):
        send_piece(0, 4, p, 2, opposite)
        send_piece(0, 2, p, 0, right)
        send_piece(0, 1, p, 1, left)
    for other in peers:
        send(sums.at[tp], sums.at[tp], send_s, recv_s.at[tp], other).start()

    wo_rows = pl.ds(pl.multiple_of(z * 128 + core * 64, 64), 64)
    wo_targets = ((2, right, 1), (1, left, 3), (3, across, 2))
    for slot, to, shift in wo_targets:
        x_to = lax.rem(x + shift, 4)
        for part, y_part in ((0, 1 - y_hi), (1, y_hi)):
            cols = pl.ds(pl.multiple_of((y_part * 4 + x_to) * FEATS, FEATS), FEATS)
            send(
                wo_in.at[wo_rows, cols],
                wo.at[slot, wo_rows, pl.ds(part * FEATS, FEATS)],
                send_wx.at[slot - 1, part],
                recv_wx.at[slot - 1, part],
                to,
            ).start()

    sends_tree = [
        [((MASKS[tree][dim] >> node) & 1) == 1 for dim in range(3)] for tree in range(3)
    ]

    def weight_tree(tree, step):
        mine = chunk(tree, step, core)
        pltpu.make_async_copy(w.at[mine], w.at[mine], recv_w.at[tree, step, core]).wait()
        for dim in range(3):
            if MASKS[tree][dim]:

                @pl.when(sends_tree[tree][dim])
                def _(dim=dim):
                    send(w.at[mine], w.at[mine], send_w.at[dim], recv_w.at[tree, step, core], dims[dim]).start()

        @pl.when(jnp.logical_or(jnp.logical_not(source_chip), core == 0))
        def _():
            send(w.at[mine], w.at[mine], send_sib, recv_w.at[tree, step, core], sibling).start()

        @pl.when(is_source)
        def _():
            theirs = chunk(tree, step, 1)
            pltpu.make_async_copy(w.at[theirs], w.at[theirs], recv_w.at[tree, step, 1]).wait()
            send(w.at[theirs], w.at[theirs], send_sib, recv_w.at[tree, step, 1], sibling).start()

    def weight_steps(low, high):
        def slot_of(slot, carry):
            for tree in range(3):
                step = slot - LAG * ((DEPTHS[tree] >> (3 * node)) & 7)

                @pl.when(jnp.logical_and(step >= 0, step < TREE_STEPS[tree]))
                def _(tree=tree, step=step):
                    weight_tree(tree, step)

            return carry

        lax.fori_loop(low, high, slot_of, 0)

    def relay_ring(h, e):
        wait_piece(4 * h + 2, e)
        send_piece(4 * h + 2, 4 * h + 3, e, 0, right)
        wait_piece(4 * h + 1, 2 + e)
        send_piece(4 * h + 1, 4 * h + 3, 2 + e, 1, left)

    def relay_opposite(p):
        wait_piece(4, p)
        send_piece(4, 6, p, 0, right)
        send_piece(4, 5, p, 1, left)

    def wo_spread():
        for slot in range(3):
            for part in range(2):
                dst = wo.at[slot + 1, wo_rows, pl.ds(part * FEATS, FEATS)]
                pltpu.make_async_copy(dst, dst, recv_wx.at[slot, part]).wait()
        block = wo.at[pl.ds(1, 3), wo_rows, :]
        for k, to in enumerate(z_others):
            send(block, block, send_wz.at[k], recv_wz.at[k], to).start()
        send(block, block, send_ws.at[3], recv_ws.at[3], sibling).start()

    weight_steps(0, 22)
    relay_ring(0, 0)
    relay_ring(0, 1)
    weight_steps(22, 28)
    relay_opposite(0)
    weight_steps(28, 32)
    relay_opposite(1)
    weight_steps(32, 36)
    relay_opposite(2)
    weight_steps(36, 40)
    relay_opposite(3)
    weight_steps(40, 48)
    relay_ring(1, 0)
    weight_steps(48, 52)
    relay_ring(1, 1)
    weight_steps(52, N_SLOTS)
    wo_spread()

    length = [lengths[0, k] for k in range(3)]
    begins = [length[0], length[0] + length[1], length[0] + length[1] + length[2]]

    def start_of(row):
        start = jnp.zeros_like(row)
        for begin in begins:
            start = jnp.where(row >= begin, begin, start)
        return start

    cosine[...], sine[...] = rope_tables(start_of, ROWS)

    for tree in range(3):

        def others(step, carry, tree=tree):
            @pl.when(jnp.logical_not(is_source))
            def _():
                theirs = chunk(tree, step, 1 - core)
                pltpu.make_async_copy(w.at[theirs], w.at[theirs], recv_w.at[tree, step, 1 - core]).wait()

            return carry

        lax.fori_loop(0, TREE_STEPS[tree], others, 0)

    acc[...] = jnp.zeros_like(acc)

    def block_dot(slot, carry):
        turn = lax.rem(slot, 4)
        h = slot // 4

        for p in range(N_PIECES):
            seen = (turn == 0) | ((turn == 2) & (p < 2)) | ((turn == 1) & (p >= 2))

            @pl.when(jnp.logical_not(seen))
            def _(p=p):
                wait_piece(slot, p)

        shift = jnp.where(turn == 2, 3, jnp.where(turn == 3, 2, turn))
        owner = lax.rem(y_hi + h, 2) * 4 + lax.rem(x + shift, 4)
        base = pl.multiple_of(owner * FEATS, FEATS)
        for n in range(3):
            cols = pl.ds(n * 256, 256)
            acc[:, cols] += jnp.dot(
                xs[slot], w[pl.ds(base, FEATS), cols], preferred_element_type=F32
            )
        return carry

    lax.fori_loop(0, 8, block_dot, 0)

    for k in range(1, N_TP):
        sender = lax.rem(tp + k, N_TP)
        pltpu.make_async_copy(sums.at[sender], sums.at[sender], recv_s.at[sender]).wait()
    total = sums[0]
    for t in range(1, N_TP):
        total = total + sums[t]
    factor = lax.rsqrt(total * (1.0 / D) + EPSILON)
    for g in range(4):
        inv[pl.ds(g * 128, 128), :] = jnp.sum(factor[g : g + 1, :] * eye, axis=1, keepdims=True) * jnp.ones(
            (1, 128), F32
        )

    def turned(value, rows):
        return value * cosine[rows, :] + pltpu.roll(value, HD // 2, axis=1) * sine[rows, :]

    def split(g, carry):
        rows = pl.ds(pl.multiple_of(g * 128, 128), 128)
        scale = inv[rows, :]
        for head in range(HEADS):
            qb[head, rows, :] = turned(acc[rows, pl.ds(head * HD, HD)] * scale, rows).astype(BF16)
        kb[rows, :] = turned(acc[rows, pl.ds(ATT_COLS, HD)] * scale, rows).astype(BF16)
        vb[rows, :] = (acc[rows, pl.ds(ATT_COLS + HD, HD)] * scale).astype(BF16)
        return carry

    lax.fori_loop(0, 4, split, 0)

    def att_rows(slot, q):
        return att.at[slot, pl.ds(q * TQ, TQ)]

    def att_half(slot, q, half):
        return att.at[slot, pl.ds(q * TQ + half * (TQ // 2), TQ // 2)]

    for q in range(N_Q):
        low = max(0, q * TQ - LONGEST)
        high = (q + 1) * TQ
        row = lax.broadcasted_iota(jnp.int32, (TQ, high - low), 0) + q * TQ
        key = lax.broadcasted_iota(jnp.int32, (TQ, high - low), 1) + low
        allowed = (key <= row) & (key >= start_of(row))
        for head in range(HEADS):
            scores = lax.dot_general(
                qb[head, pl.ds(q * TQ, TQ), :],
                kb[pl.ds(low, high - low), :],
                (((1,), (1,)), ((), ())),
                preferred_element_type=F32,
            ) * (1.0 / math.sqrt(HD))
            scores = jnp.where(allowed, scores, -1e30)
            largest = jnp.max(scores, axis=1, keepdims=True)
            weights = jnp.exp(jnp.where(allowed, scores - largest, -1e30))
            denominator = jnp.sum(weights, axis=1, keepdims=True)
            mixed = jnp.dot(weights.astype(BF16), vb[pl.ds(low, high - low), :], preferred_element_type=F32)
            att[0, pl.ds(q * TQ, TQ), pl.ds(head * HD, HD)] = (mixed / denominator).astype(BF16)
        send(att_rows(0, q), att_rows(2, q), send_a.at[0], recv_a.at[1, q], right).start()
        send(att_rows(0, q), att_rows(1, q), send_a.at[1], recv_a.at[0, q], left).start()

    for copy in wo_local:
        copy.wait()
    for k in range(3):
        z_from = lax.rem(z + 3 - k, 4)
        rows = pl.ds(pl.multiple_of(z_from * 128 + core * 64, 64), 64)
        block = wo.at[pl.ds(1, 3), rows, :]
        pltpu.make_async_copy(block, block, recv_wz.at[k]).wait()
        send(block, block, send_ws.at[k], recv_ws.at[k], sibling).start()
    for k in range(4):
        z_from = lax.rem(z + 3 - k, 4)
        rows = pl.ds(pl.multiple_of(z_from * 128 + (1 - core) * 64, 64), 64)
        block = wo.at[pl.ds(1, 3), rows, :]
        pltpu.make_async_copy(block, block, recv_ws.at[k]).wait()

    def relay_att(q):
        pltpu.make_async_copy(att_rows(2, q), att_rows(2, q), recv_a.at[1, q]).wait()
        send(att_half(2, q, 0), att_half(3, q, 0), send_a.at[0], recv_a.at[2, q], right).start()
        pltpu.make_async_copy(att_rows(1, q), att_rows(1, q), recv_a.at[0, q]).wait()
        send(att_half(1, q, 1), att_half(3, q, 1), send_a.at[1], recv_a.at[3, q], left).start()

    def finish(q):
        for half in range(2):
            pltpu.make_async_copy(att_half(3, q, half), att_half(3, q, half), recv_a.at[2 + half, q]).wait()

        def tile(cols):
            total = jnp.dot(att[0, pl.ds(q * TQ, TQ), :], wo[0, :, cols], preferred_element_type=F32)
            for slot in range(1, 4):
                total += jnp.dot(att[slot, pl.ds(q * TQ, TQ), :], wo[slot, :, cols], preferred_element_type=F32)
            return total

        def foreign(n, carry):
            cols = pl.ds(pl.multiple_of(n * 256, 256), 256)
            pf[pl.ds(q * TQ, TQ), cols] = tile(cols).astype(BF16)
            return carry

        def mine(n, carry):
            cols = pl.ds(pl.multiple_of(n * 256, 256), 256)
            own[pl.ds(q * TQ, TQ), cols] = tile(pl.ds(pl.multiple_of(FEATS + n * 256, 256), 256))
            return carry

        lax.fori_loop(0, 4, foreign, 0)
        send(
            pf.at[pl.ds(q * TQ, TQ)], rb.at[pl.ds(q * TQ, TQ)], send_y, recv_y.at[q], opposite
        ).start()
        lax.fori_loop(0, 4, mine, 0)

    relay_att(0)
    for q in range(N_Q):
        if q + 1 < N_Q:
            relay_att(q + 1)
        finish(q)
    for q in range(N_Q):
        rows = pl.ds(q * TQ, TQ)
        pltpu.make_async_copy(rb.at[rows], rb.at[rows], recv_y.at[q]).wait()
        out[rows, :] = (own[rows, :] + rb[rows, :].astype(F32)).astype(BF16)

    for tree in range(3):
        half = pl.ds(0, TREE_STEPS[tree] * CHUNK)
        for dim in range(3):
            if MASKS[tree][dim]:

                @pl.when(sends_tree[tree][dim])
                def _(half=half, dim=dim):
                    pltpu.make_async_copy(w.at[half], w.at[half], send_w.at[dim]).wait()

    @pl.when(is_source)
    def _():
        pltpu.make_async_copy(w, w, send_sib).wait()

    @pl.when(jnp.logical_not(source_chip))
    def _():
        half = w.at[pl.ds(0, D // 2)]
        pltpu.make_async_copy(half, half, send_sib).wait()

    for side in range(2):
        pltpu.make_async_copy(xs.at[pl.ds(0, 3)], xs.at[pl.ds(0, 3)], send_x.at[side]).wait()
    pltpu.make_async_copy(xs.at[0], xs.at[0], send_x.at[2]).wait()
    pltpu.make_async_copy(sums.at[pl.ds(0, 7)], sums.at[pl.ds(0, 7)], send_s).wait()
    for slot in range(3):
        for part in range(2):
            dst = wo.at[0, pl.ds(0, 64), pl.ds(0, FEATS)]
            pltpu.make_async_copy(dst, dst, send_wx.at[slot, part]).wait()
    block = wo.at[pl.ds(1, 3), pl.ds(0, 64), :]
    for k in range(3):
        pltpu.make_async_copy(block, block, send_wz.at[k]).wait()
    for k in range(4):
        pltpu.make_async_copy(block, block, send_ws.at[k]).wait()
    for side in range(2):
        sent = att.at[0, :, :]
        pltpu.make_async_copy(sent, sent, send_a.at[side]).wait()
        sent = att.at[0, pl.ds(0, ROWS // 2)]
        pltpu.make_async_copy(sent, sent, send_a.at[side]).wait()
    pltpu.make_async_copy(pf, pf, send_y).wait()


def local(hidden_rows, lengths, attn_gain, w_joined, w_out):
    tp = lax.axis_index("tp")
    gain = lax.dynamic_slice(attn_gain, (tp * FEATS,), (FEATS,)).reshape(1, FEATS)
    dma = pltpu.SemaphoreType.DMA
    vmem = pl.BlockSpec(memory_space=pltpu.VMEM)
    anywhere = pl.BlockSpec(memory_space=pl.ANY)
    return pl.pallas_call(
        body,
        out_shape=jax.ShapeDtypeStruct((ROWS, FEATS), BF16),
        in_specs=[vmem, pl.BlockSpec(memory_space=pltpu.SMEM), vmem, anywhere, anywhere],
        out_specs=vmem,
        scratch_shapes=[
            pltpu.VMEM((D, COLS), BF16),
            pltpu.VMEM((8, ROWS, FEATS), BF16),
            pltpu.VMEM((4, ATT_COLS, 2 * FEATS), BF16),
            pltpu.VMEM((ROWS, COLS), F32),
            pltpu.VMEM((4, ROWS, ATT_COLS), BF16),
            pltpu.VMEM((ROWS, FEATS), BF16),
            pltpu.VMEM((ROWS, FEATS), BF16),
            pltpu.VMEM((ROWS, FEATS), F32),
            pltpu.VMEM((N_TP, 8, 128), F32),
            pltpu.VMEM((ROWS, 128), F32),
            pltpu.VMEM((ROWS, HD), F32),
            pltpu.VMEM((ROWS, HD), F32),
            pltpu.VMEM((HEADS, ROWS, HD), BF16),
            pltpu.VMEM((ROWS, HD), BF16),
            pltpu.VMEM((ROWS, HD), BF16),
            dma((3, max(TREE_STEPS), 2)),
            dma((3,)),
            dma,
            dma((8, N_PIECES)),
            dma((3,)),
            dma((N_TP,)),
            dma,
            dma((3, 2)),
            dma((3, 2)),
            dma((3,)),
            dma((3,)),
            dma((4,)),
            dma((4,)),
            dma((2,)),
            dma((4, N_Q)),
            dma((2,)),
            dma((N_Q,)),
            dma,
        ],
        compiler_params=pltpu.CompilerParams(
            collective_id=0, has_side_effects=True, vmem_limit_bytes=56 * 1024 * 1024
        ),
    )(hidden_rows, lengths, gain, w_joined, w_out)


def solution(mesh):
    return jax.shard_map(
        local,
        mesh=mesh,
        in_specs=(P("inst", "tp"), P("inst", None), P(), P("inst", None, "tp"), P("tp", None)),
        out_specs=P("inst", "tp"),
        check_vma=False,
    )
```

```python
import functools
import math

import jax
import jax.numpy as jnp
from jax import lax
from jax.experimental import pallas as pl
from jax.experimental.pallas import tpu as pltpu
from jax.sharding import PartitionSpec as P

MESH = pl.DeviceIdType.MESH
F32 = jnp.float32
BF16 = jnp.bfloat16

KVHEADS = 8
HD = 128
QHEADS = 32
ROWS = 512
D = 8192
N_TP = 8
FEATS = D // N_TP
COLS = 768
HEADS = QHEADS // N_TP
ATT_COLS = HEADS * HD
LONGEST = 256

EPSILON = 1e-05
ROPE_BASE = 500000.0
ROPE_FACTOR = 8.0
LOW_FACTOR = 1.0
HIGH_FACTOR = 4.0
OLD_CONTEXT = 8192.0

CHUNK = 64
TREE_STEPS = (44, 44, 40)
TREE_BASE = (0, 2816, 5632)
GRAY = (0, 1, 3, 2)
LAG = 4
AHEAD = 4
N_SLOTS = max(TREE_STEPS) + 4 * LAG

Y_FIRST = (0, 1)
PIECE = 128
N_PIECES = ROWS // PIECE
TQ = 128
N_Q = ROWS // TQ


def tree_masks():
    masks = [[0] * 3 for _ in range(3)]
    depths = [0] * 3
    node_of = {}
    for y_lo in range(2):
        for z in range(4):
            node_of[y_lo * 4 + GRAY[z]] = y_lo * 4 + z
    first_edges = [(0, 0), (1, 1), (1, 2), (3, 2), (3, 0), (5, 0), (7, 0)]
    for tree in range(3):
        depth = {0: 0}
        for code, dim in first_edges:
            depth[code ^ (1 << dim)] = depth[code] + 1
            turned = ((code << tree) | (code >> (3 - tree))) & 7
            if code:
                masks[tree][(dim + tree) % 3] |= 1 << node_of[turned]
        for code, far in depth.items():
            turned = ((code << tree) | (code >> (3 - tree))) & 7
            depths[tree] |= far << (3 * node_of[turned])
    return masks, depths


MASKS, DEPTHS = tree_masks()


def rope_tables(start_of, rows):
    lane = lax.broadcasted_iota(jnp.int32, (1, HD), 1)
    index = lax.rem(lane, HD // 2).astype(F32)
    base = jnp.exp(index * (-2.0 * math.log(ROPE_BASE) / HD))
    wavelength = 2.0 * math.pi / base
    blending = (OLD_CONTEXT / wavelength - LOW_FACTOR) / (HIGH_FACTOR - LOW_FACTOR)
    blended = (1.0 - blending) * base / ROPE_FACTOR + blending * base
    slowed = jnp.where(wavelength > OLD_CONTEXT / LOW_FACTOR, base / ROPE_FACTOR, blended)
    frequency = jnp.where(wavelength < OLD_CONTEXT / HIGH_FACTOR, base, slowed)
    row = lax.broadcasted_iota(jnp.int32, (rows, HD), 0)
    angles = (row - start_of(row)).astype(F32) * frequency
    sine = jnp.sin(angles)
    return jnp.cos(angles), jnp.where(lane < HD // 2, -sine, sine)


def body(
    hidden, lengths, gain, w_in, wo_in, out,
    w, xs, xl, wo, acc, att, pf, rb, own, sums, inv, cosine, sine, qb, kb, vb,
    recv_w, send_w, send_r, send_sib, recv_x, recv_l, send_x, recv_s, send_s,
    recv_wx, send_wx, recv_wz, send_wz, recv_ws, send_ws, loc_wo,
    recv_a, send_a, recv_y, send_y,
):
    inst = lax.axis_index("inst")
    tp = lax.axis_index("tp")
    core = lax.rem(inst, 2)
    z = lax.rem(inst // 2, 4)
    y_lo = inst // 8
    x = lax.rem(tp, 4)
    y_hi = tp // 4

    def inst_of(y_lo_, z_, core_):
        return (y_lo_ * 4 + z_) * 2 + core_

    tp_right = y_hi * 4 + lax.rem(x + 1, 4)
    tp_left = y_hi * 4 + lax.rem(x + 3, 4)
    right = (inst, tp_right)
    left = (inst, tp_left)
    tp_opposite = (1 - y_hi) * 4 + x
    opposite = (inst, tp_opposite)
    other_inst = inst_of(y_lo, z, 1 - core)
    sibling = (other_inst, tp)
    right_other = (other_inst, tp_right)
    left_other = (other_inst, tp_left)
    across_other = (other_inst, y_hi * 4 + lax.rem(x + 2, 4))
    dims = (
        (inst_of(y_lo, z + 1 - 2 * lax.rem(z, 2), core), tp),
        (inst_of(y_lo, 3 - z, core), tp),
        (inst_of(1 - y_lo, z, core), tp),
    )
    z_others = [(inst_of(y_lo, lax.rem(z + k, 4), core), tp) for k in (1, 2, 3)]
    node = y_lo * 4 + z
    source_chip = node == 0
    is_source = jnp.logical_and(source_chip, core == 0)
    relays_w = core == 0
    relays_x = core == 1

    def send(src, dst, s_sem, r_sem, to):
        return pltpu.make_async_remote_copy(
            src_ref=src, dst_ref=dst, send_sem=s_sem, recv_sem=r_sem, device_id=to, device_id_type=MESH
        )

    def chunk(tree, step):
        at = TREE_BASE[tree] + step * CHUNK
        return pl.ds(pl.multiple_of(at, CHUNK), CHUNK)

    barrier = pltpu.get_barrier_semaphore()
    peers = [(inst, lax.rem(tp + k, N_TP)) for k in range(1, N_TP)]
    greeted = peers + z_others + [sibling, dims[2], right_other, left_other, across_other]
    for other in greeted:
        pl.semaphore_signal(barrier, inc=1, device_id=other, device_id_type=MESH)

    @pl.when(is_source)
    def _():
        for tree in range(3):

            def load(step, carry, tree=tree):
                rows = chunk(tree, step)
                pltpu.make_async_copy(w_in.at[0, rows], w.at[rows], recv_w.at[tree, step]).start()
                return carry

            lax.fori_loop(0, TREE_STEPS[tree], load, 0)

    foreign_cols = pl.ds(pl.multiple_of(((1 - y_hi) * 4 + x) * FEATS, FEATS), FEATS)
    own_cols = pl.ds(pl.multiple_of(tp * FEATS, FEATS), FEATS)
    wo_local = (
        pltpu.make_async_copy(wo_in.at[:, foreign_cols], wo.at[0, :, pl.ds(0, FEATS)], loc_wo.at[0]),
        pltpu.make_async_copy(wo_in.at[:, own_cols], wo.at[0, :, pl.ds(FEATS, FEATS)], loc_wo.at[1]),
    )
    for copy in wo_local:
        copy.start()

    eye = (
        lax.broadcasted_iota(jnp.int32, (128, 128), 0) == lax.broadcasted_iota(jnp.int32, (128, 128), 1)
    ).astype(F32)
    sums[tp] = jnp.zeros((8, 128), F32)
    for g in range(4):
        wide = hidden[pl.ds(g * 128, 128), :].astype(F32)
        xs[0, pl.ds(g * 128, 128), :] = (wide * gain[pl.ds(tp, 1), :]).astype(BF16)
        column = jnp.sum(wide * wide, axis=1, keepdims=True)
        sums[tp, pl.ds(g, 1), :] = jnp.sum(column * eye, axis=0, keepdims=True)

    pl.semaphore_wait(barrier, len(greeted))

    def piece(slot, p):
        return xs.at[slot, pl.ds(p * PIECE, PIECE)]

    def landed(block, p):
        return xl.at[block, pl.ds(p * PIECE, PIECE)]

    def send_piece(src, dst, sem, r_sem, to):
        send(src, dst, send_x.at[sem], r_sem, to).start()

    def wait_piece(slot, p):
        pltpu.make_async_copy(piece(slot, p), piece(slot, p), recv_x.at[slot, p]).wait()

    def wait_landed(block, p):
        pltpu.make_async_copy(landed(block, p), landed(block, p), recv_l.at[block, p]).wait()

    def to_final(src, slot, p, sem, to):
        send_piece(src, piece(slot, p), sem, recv_x.at[slot, p], to)

    def to_relay(src, block, p, sem, to):
        send_piece(src, landed(block, p), sem, recv_l.at[block, p], to)

    def cross(p):
        to_final(piece(0, p), 4, p, 2, opposite)
        to_relay(landed(3, p), 1, p, 2, opposite)

    @pl.when(relays_w)
    def _():
        for p in range(N_PIECES):
            to_relay(piece(0, p), 3, p, 2, sibling)

    @pl.when(relays_x)
    def _():
        for p in range(N_PIECES):
            to_final(piece(0, p), 2, p, 0, right)
            to_final(piece(0, p), 1, p, 1, left)
            wait_landed(3, p)
            if p % 2 == 0:
                to_relay(landed(3, p), 0, p, 0, right)
                to_final(landed(3, p), 1, p, 1, left_other)
            else:
                to_final(landed(3, p), 2, p, 0, right_other)
                to_relay(landed(3, p), 0, p, 1, left)
            if p in Y_FIRST:
                cross(p)

    for other in peers:
        send(sums.at[tp], sums.at[tp], send_s, recv_s.at[tp], other).start()

    wo_rows = pl.ds(pl.multiple_of(z * 128, 128), 128)
    wo_targets = ((2, right_other, 1), (1, left_other, 3), (3, across_other, 2))

    def wo_sends():
        for slot, to, shift in wo_targets:
            x_to = lax.rem(x + shift, 4)
            for part, y_part in ((0, 1 - y_hi), (1, y_hi)):
                cols = pl.ds(pl.multiple_of((y_part * 4 + x_to) * FEATS, FEATS), FEATS)
                send(
                    wo_in.at[wo_rows, cols],
                    wo.at[slot, wo_rows, pl.ds(part * FEATS, FEATS)],
                    send_wx.at[slot - 1, part],
                    recv_wx.at[slot - 1, part],
                    to,
                ).start()

    sends_tree = [
        [((MASKS[tree][dim] >> node) & 1) == 1 for dim in range(3)] for tree in range(3)
    ]

    def weight_tree(tree, step):
        rows = chunk(tree, step)
        pltpu.make_async_copy(w.at[rows], w.at[rows], recv_w.at[tree, step]).wait()
        for dim in range(3):
            if MASKS[tree][dim]:

                @pl.when(sends_tree[tree][dim])
                def _(dim=dim):
                    send(w.at[rows], w.at[rows], send_w.at[dim], recv_w.at[tree, step], dims[dim]).start()

        @pl.when(is_source)
        def _():
            turn = lax.rem(step, AHEAD)

            @pl.when(step >= AHEAD)
            def _():
                pltpu.make_async_copy(w.at[rows], w.at[rows], send_r.at[tree, turn]).wait()

            send(w.at[rows], w.at[rows], send_r.at[tree, turn], recv_w.at[tree, step], dims[tree]).start()

        send(w.at[rows], w.at[rows], send_sib, recv_w.at[tree, step], sibling).start()

    def wo_arrived():
        for slot in range(3):
            for part in range(2):
                dst = wo.at[slot + 1, wo_rows, pl.ds(part * FEATS, FEATS)]
                pltpu.make_async_copy(dst, dst, recv_wx.at[slot, part]).wait()
        block = wo.at[pl.ds(1, 3), wo_rows, :]
        send(block, block, send_ws.at[3], recv_ws.at[3], sibling).start()

        for k, to in enumerate(z_others):
            send(block, block, send_wz.at[k], recv_wz.at[k], to).start()

    def weight_steps():
        def slot_of(slot, carry):
            for tree in range(3):
                step = slot - LAG * ((DEPTHS[tree] >> (3 * node)) & 7)

                @pl.when(jnp.logical_and(step >= 0, step < TREE_STEPS[tree]))
                def _(tree=tree, step=step):
                    weight_tree(tree, step)

            return carry

        lax.fori_loop(0, N_SLOTS, slot_of, 0)

    def relay_ring(h, e):
        p = 2 * e
        wait_piece(4 * h + 2, p)
        to_final(piece(4 * h + 2, p), 4 * h + 3, p, 0, right)
        wait_landed(2 * h, p)
        to_final(landed(2 * h, p), 4 * h + 3, p, 0, right_other)
        to_final(landed(2 * h, p), 4 * h + 2, p, 3, sibling)
        p = 2 * e + 1
        wait_piece(4 * h + 1, p)
        to_final(piece(4 * h + 1, p), 4 * h + 3, p, 1, left)
        wait_landed(2 * h, p)
        to_final(landed(2 * h, p), 4 * h + 3, p, 1, left_other)
        to_final(landed(2 * h, p), 4 * h + 1, p, 3, sibling)

    def relay_opposite(p):
        wait_piece(4, p)
        to_final(piece(4, p), 6, p, 0, right)
        to_final(piece(4, p), 5, p, 1, left)
        wait_landed(1, p)
        if p % 2 == 0:
            to_relay(landed(1, p), 2, p, 0, right)
            to_final(landed(1, p), 5, p, 1, left_other)
        else:
            to_final(landed(1, p), 6, p, 0, right_other)
            to_relay(landed(1, p), 2, p, 1, left)
        to_final(landed(1, p), 4, p, 3, sibling)

    @pl.when(relays_w)
    def _():
        weight_steps()
        wo_arrived()

    @pl.when(relays_x)
    def _():
        relay_ring(0, 0)
        relay_ring(0, 1)
        wo_sends()
        relay_opposite(0)
        relay_opposite(1)
        relay_ring(1, 0)
        for p in range(N_PIECES):
            if p not in Y_FIRST:
                cross(p)
        relay_opposite(2)
        relay_opposite(3)
        relay_ring(1, 1)

    length = [lengths[0, k] for k in range(3)]
    begins = [length[0], length[0] + length[1], length[0] + length[1] + length[2]]

    def start_of(row):
        start = jnp.zeros_like(row)
        for begin in begins:
            start = jnp.where(row >= begin, begin, start)
        return start

    cosine[...], sine[...] = rope_tables(start_of, ROWS)

    @pl.when(relays_x)
    def _():
        for tree in range(3):

            def passed(step, carry, tree=tree):
                rows = chunk(tree, step)
                pltpu.make_async_copy(w.at[rows], w.at[rows], recv_w.at[tree, step]).wait()
                return carry

            lax.fori_loop(0, TREE_STEPS[tree], passed, 0)

    acc[...] = jnp.zeros_like(acc)

    def block_dot(slot, carry):
        turn = lax.rem(slot, 4)
        h = slot // 4

        for p in range(N_PIECES):
            relayed = (turn == 0) | ((turn == 2) & (p % 2 == 0)) | ((turn == 1) & (p % 2 == 1))
            seen = (slot == 0) | (relays_x & relayed)

            @pl.when(jnp.logical_not(seen))
            def _(p=p):
                wait_piece(slot, p)

        shift = jnp.where(turn == 2, 3, jnp.where(turn == 3, 2, turn))
        owner = lax.rem(y_hi + h, 2) * 4 + lax.rem(x + shift, 4)
        base = pl.multiple_of(owner * FEATS, FEATS)
        for n in range(3):
            cols = pl.ds(n * 256, 256)
            acc[:, cols] += jnp.dot(
                xs[slot], w[pl.ds(base, FEATS), cols], preferred_element_type=F32
            )
        return carry

    lax.fori_loop(0, 8, block_dot, 0)

    for k in range(1, N_TP):
        sender = lax.rem(tp + k, N_TP)
        pltpu.make_async_copy(sums.at[sender], sums.at[sender], recv_s.at[sender]).wait()
    total = sums[0]
    for t in range(1, N_TP):
        total = total + sums[t]
    factor = lax.rsqrt(total * (1.0 / D) + EPSILON)
    for g in range(4):
        inv[pl.ds(g * 128, 128), :] = jnp.sum(factor[g : g + 1, :] * eye, axis=1, keepdims=True) * jnp.ones(
            (1, 128), F32
        )

    def turned(value, rows):
        return value * cosine[rows, :] + pltpu.roll(value, HD // 2, axis=1) * sine[rows, :]

    def split(g, carry):
        rows = pl.ds(pl.multiple_of(g * 128, 128), 128)
        scale = inv[rows, :]
        for head in range(HEADS):
            qb[head, rows, :] = turned(acc[rows, pl.ds(head * HD, HD)] * scale, rows).astype(BF16)
        kb[rows, :] = turned(acc[rows, pl.ds(ATT_COLS, HD)] * scale, rows).astype(BF16)
        vb[rows, :] = (acc[rows, pl.ds(ATT_COLS + HD, HD)] * scale).astype(BF16)
        return carry

    lax.fori_loop(0, 4, split, 0)

    def att_rows(slot, q):
        return att.at[slot, pl.ds(q * TQ, TQ)]

    def att_half(slot, q, half):
        return att.at[slot, pl.ds(q * TQ + half * (TQ // 2), TQ // 2)]

    def wo_pass(k):
        z_from = lax.rem(z + 3 - k, 4)
        block = wo.at[pl.ds(1, 3), pl.ds(pl.multiple_of(z_from * 128, 128), 128), :]
        pltpu.make_async_copy(block, block, recv_wz.at[k]).wait()
        send(block, block, send_ws.at[k], recv_ws.at[k], sibling).start()

    for q in range(N_Q):
        low = max(0, q * TQ - LONGEST)
        high = (q + 1) * TQ
        row = lax.broadcasted_iota(jnp.int32, (TQ, high - low), 0) + q * TQ
        key = lax.broadcasted_iota(jnp.int32, (TQ, high - low), 1) + low
        allowed = (key <= row) & (key >= start_of(row))
        for head in range(HEADS):
            scores = lax.dot_general(
                qb[head, pl.ds(q * TQ, TQ), :],
                kb[pl.ds(low, high - low), :],
                (((1,), (1,)), ((), ())),
                preferred_element_type=F32,
            ) * (1.0 / math.sqrt(HD))
            scores = jnp.where(allowed, scores, -1e30)
            largest = jnp.max(scores, axis=1, keepdims=True)
            weights = jnp.exp(jnp.where(allowed, scores - largest, -1e30))
            denominator = jnp.sum(weights, axis=1, keepdims=True)
            mixed = jnp.dot(weights.astype(BF16), vb[pl.ds(low, high - low), :], preferred_element_type=F32)
            att[0, pl.ds(q * TQ, TQ), pl.ds(head * HD, HD)] = (mixed / denominator).astype(BF16)
        send(att_rows(0, q), att_rows(2, q), send_a.at[0], recv_a.at[1, q], right).start()
        send(att_rows(0, q), att_rows(1, q), send_a.at[1], recv_a.at[0, q], left).start()

    @pl.when(relays_w)
    def _():
        for k in (0, 2, 1):
            wo_pass(k)

    for copy in wo_local:
        copy.wait()
    @pl.when(relays_x)
    def _():
        for k in range(4):
            z_from = lax.rem(z + 3 - k, 4)
            block = wo.at[pl.ds(1, 3), pl.ds(pl.multiple_of(z_from * 128, 128), 128), :]
            pltpu.make_async_copy(block, block, recv_ws.at[k]).wait()

    def relay_att(q):
        pltpu.make_async_copy(att_rows(2, q), att_rows(2, q), recv_a.at[1, q]).wait()
        send(att_half(2, q, 0), att_half(3, q, 0), send_a.at[0], recv_a.at[2, q], right).start()
        pltpu.make_async_copy(att_rows(1, q), att_rows(1, q), recv_a.at[0, q]).wait()
        send(att_half(1, q, 1), att_half(3, q, 1), send_a.at[1], recv_a.at[3, q], left).start()

    def finish(q):
        for half in range(2):
            pltpu.make_async_copy(att_half(3, q, half), att_half(3, q, half), recv_a.at[2 + half, q]).wait()

        def tile(cols):
            total = jnp.dot(att[0, pl.ds(q * TQ, TQ), :], wo[0, :, cols], preferred_element_type=F32)
            for slot in range(1, 4):
                total += jnp.dot(att[slot, pl.ds(q * TQ, TQ), :], wo[slot, :, cols], preferred_element_type=F32)
            return total

        def foreign(n, carry):
            cols = pl.ds(pl.multiple_of(n * 256, 256), 256)
            pf[pl.ds(q * TQ, TQ), cols] = tile(cols).astype(BF16)
            return carry

        def mine(n, carry):
            cols = pl.ds(pl.multiple_of(n * 256, 256), 256)
            own[pl.ds(q * TQ, TQ), cols] = tile(pl.ds(pl.multiple_of(FEATS + n * 256, 256), 256))
            return carry

        lax.fori_loop(0, 4, foreign, 0)
        send(
            pf.at[pl.ds(q * TQ, TQ)], rb.at[pl.ds(q * TQ, TQ)], send_y, recv_y.at[q], opposite
        ).start()
        lax.fori_loop(0, 4, mine, 0)

    relay_att(0)
    for q in range(N_Q):
        if q + 1 < N_Q:
            relay_att(q + 1)
        finish(q)
    for q in range(N_Q):
        rows = pl.ds(q * TQ, TQ)
        pltpu.make_async_copy(rb.at[rows], rb.at[rows], recv_y.at[q]).wait()
        out[rows, :] = (own[rows, :] + rb[rows, :].astype(F32)).astype(BF16)

    def sent(ref, sem):
        pltpu.make_async_copy(ref, ref, sem).wait()

    @pl.when(relays_w)
    def _():
        for tree in range(3):
            for dim in range(3):
                if MASKS[tree][dim]:

                    @pl.when(sends_tree[tree][dim])
                    def _(tree=tree, dim=dim):
                        sent(w.at[pl.ds(0, TREE_STEPS[tree] * CHUNK)], send_w.at[dim])

        @pl.when(is_source)
        def _():
            for tree in range(3):
                for turn in range(AHEAD):
                    sent(w.at[pl.ds(0, CHUNK)], send_r.at[tree, turn])

        sent(w, send_sib)
        sent(xs.at[0], send_x.at[2])
        block = wo.at[pl.ds(1, 3), pl.ds(0, 128), :]
        for k in range(3):
            sent(block, send_wz.at[k])
        for k in range(4):
            sent(block, send_ws.at[k])

    @pl.when(relays_x)
    def _():
        for side in range(2):
            sent(xs.at[pl.ds(0, 6)], send_x.at[side])
        sent(xs.at[pl.ds(0, 2)], send_x.at[2])
        sent(xs.at[pl.ds(0, 3)], send_x.at[3])
        for slot in range(3):
            for part in range(2):
                sent(wo.at[0, pl.ds(0, 128), pl.ds(0, FEATS)], send_wx.at[slot, part])

    sent(sums.at[pl.ds(0, 7)], send_s)
    for side in range(2):
        sent(att.at[0], send_a.at[side])
        sent(att.at[0, pl.ds(0, ROWS // 2)], send_a.at[side])
    sent(pf, send_y)


def local(hidden_rows, lengths, attn_gain, w_joined, w_out):
    gain = attn_gain.reshape(N_TP, FEATS)
    dma = pltpu.SemaphoreType.DMA
    vmem = pl.BlockSpec(memory_space=pltpu.VMEM)
    anywhere = pl.BlockSpec(memory_space=pl.ANY)
    return pl.pallas_call(
        body,
        out_shape=jax.ShapeDtypeStruct((ROWS, FEATS), BF16),
        in_specs=[vmem, pl.BlockSpec(memory_space=pltpu.SMEM), vmem, anywhere, anywhere],
        out_specs=vmem,
        scratch_shapes=[
            pltpu.VMEM((D, COLS), BF16),
            pltpu.VMEM((8, ROWS, FEATS), BF16),
            pltpu.VMEM((4, ROWS, FEATS), BF16),
            pltpu.VMEM((4, ATT_COLS, 2 * FEATS), BF16),
            pltpu.VMEM((ROWS, COLS), F32),
            pltpu.VMEM((4, ROWS, ATT_COLS), BF16),
            pltpu.VMEM((ROWS, FEATS), BF16),
            pltpu.VMEM((ROWS, FEATS), BF16),
            pltpu.VMEM((ROWS, FEATS), F32),
            pltpu.VMEM((N_TP, 8, 128), F32),
            pltpu.VMEM((ROWS, 128), F32),
            pltpu.VMEM((ROWS, HD), F32),
            pltpu.VMEM((ROWS, HD), F32),
            pltpu.VMEM((HEADS, ROWS, HD), BF16),
            pltpu.VMEM((ROWS, HD), BF16),
            pltpu.VMEM((ROWS, HD), BF16),
            dma((3, max(TREE_STEPS))),
            dma((3,)),
            dma((3, AHEAD)),
            dma,
            dma((8, N_PIECES)),
            dma((4, N_PIECES)),
            dma((4,)),
            dma((N_TP,)),
            dma,
            dma((3, 2)),
            dma((3, 2)),
            dma((3,)),
            dma((3,)),
            dma((4,)),
            dma((4,)),
            dma((2,)),
            dma((4, N_Q)),
            dma((2,)),
            dma((N_Q,)),
            dma,
        ],
        compiler_params=pltpu.CompilerParams(
            collective_id=0, has_side_effects=True, vmem_limit_bytes=56 * 1024 * 1024
        ),
    )(hidden_rows, lengths, gain, w_joined, w_out)


def solution(mesh):
    return jax.shard_map(
        local,
        mesh=mesh,
        in_specs=(P("inst", "tp"), P("inst", None), P(), P("inst", None, "tp"), P("tp", None)),
        out_specs=P("inst", "tp"),
        check_vma=False,
    )
```

```python
import functools
import math

import jax
import jax.numpy as jnp
from jax import lax
from jax.experimental import pallas as pl
from jax.experimental.pallas import tpu as pltpu
from jax.sharding import PartitionSpec as P

MESH = pl.DeviceIdType.MESH
F32 = jnp.float32
BF16 = jnp.bfloat16

KVHEADS = 8
HD = 128
QHEADS = 32
ROWS = 512
D = 8192
N_TP = 8
FEATS = D // N_TP
COLS = 768
HEADS = QHEADS // N_TP
ATT_COLS = HEADS * HD
LONGEST = 256

EPSILON = 1e-05
ROPE_BASE = 500000.0
ROPE_FACTOR = 8.0
LOW_FACTOR = 1.0
HIGH_FACTOR = 4.0
OLD_CONTEXT = 8192.0

CHUNK = 64
TREE_STEPS = (44, 44, 40)
TREE_BASE = (0, 2816, 5632)
GRAY = (0, 1, 3, 2)
LAG = 4
AHEAD = 4
N_SLOTS = max(TREE_STEPS) + 4 * LAG

Y_FIRST = (0, 1, 2)
PIECE = 128
N_PIECES = ROWS // PIECE
TQ = 128
N_Q = ROWS // TQ


def tree_masks():
    masks = [[0] * 3 for _ in range(3)]
    depths = [0] * 3
    node_of = {}
    for y_lo in range(2):
        for z in range(4):
            node_of[y_lo * 4 + GRAY[z]] = y_lo * 4 + z
    first_edges = [(0, 0), (1, 1), (1, 2), (3, 2), (3, 0), (5, 0), (7, 0)]
    for tree in range(3):
        depth = {0: 0}
        for code, dim in first_edges:
            depth[code ^ (1 << dim)] = depth[code] + 1
            turned = ((code << tree) | (code >> (3 - tree))) & 7
            if code:
                masks[tree][(dim + tree) % 3] |= 1 << node_of[turned]
        for code, far in depth.items():
            turned = ((code << tree) | (code >> (3 - tree))) & 7
            depths[tree] |= far << (3 * node_of[turned])
    return masks, depths


MASKS, DEPTHS = tree_masks()


def rope_tables(start_of, rows):
    lane = lax.broadcasted_iota(jnp.int32, (1, HD), 1)
    index = lax.rem(lane, HD // 2).astype(F32)
    base = jnp.exp(index * (-2.0 * math.log(ROPE_BASE) / HD))
    wavelength = 2.0 * math.pi / base
    blending = (OLD_CONTEXT / wavelength - LOW_FACTOR) / (HIGH_FACTOR - LOW_FACTOR)
    blended = (1.0 - blending) * base / ROPE_FACTOR + blending * base
    slowed = jnp.where(wavelength > OLD_CONTEXT / LOW_FACTOR, base / ROPE_FACTOR, blended)
    frequency = jnp.where(wavelength < OLD_CONTEXT / HIGH_FACTOR, base, slowed)
    row = lax.broadcasted_iota(jnp.int32, (rows, HD), 0)
    angles = (row - start_of(row)).astype(F32) * frequency
    sine = jnp.sin(angles)
    return jnp.cos(angles), jnp.where(lane < HD // 2, -sine, sine)


def body(
    hidden, lengths, gain, w_in, wo_in, out,
    w, xs, xl, wo, acc, att, pf, rb, own, sums, inv, cosine, sine, qb, kb, vb,
    recv_w, send_w, send_r, send_sib, recv_x, recv_l, send_x, recv_s, send_s,
    recv_wx, send_wx, recv_wz, send_wz, recv_ws, send_ws, loc_wo,
    recv_a, send_a, recv_y, send_y,
):
    inst = lax.axis_index("inst")
    tp = lax.axis_index("tp")
    core = lax.rem(inst, 2)
    z = lax.rem(inst // 2, 4)
    y_lo = inst // 8
    x = lax.rem(tp, 4)
    y_hi = tp // 4

    def inst_of(y_lo_, z_, core_):
        return (y_lo_ * 4 + z_) * 2 + core_

    tp_right = y_hi * 4 + lax.rem(x + 1, 4)
    tp_left = y_hi * 4 + lax.rem(x + 3, 4)
    right = (inst, tp_right)
    left = (inst, tp_left)
    tp_opposite = (1 - y_hi) * 4 + x
    opposite = (inst, tp_opposite)
    other_inst = inst_of(y_lo, z, 1 - core)
    sibling = (other_inst, tp)
    right_other = (other_inst, tp_right)
    left_other = (other_inst, tp_left)
    across_other = (other_inst, y_hi * 4 + lax.rem(x + 2, 4))
    dims = (
        (inst_of(y_lo, z + 1 - 2 * lax.rem(z, 2), core), tp),
        (inst_of(y_lo, 3 - z, core), tp),
        (inst_of(1 - y_lo, z, core), tp),
    )
    z_others = [(inst_of(y_lo, lax.rem(z + k, 4), core), tp) for k in (1, 2, 3)]
    node = y_lo * 4 + z
    source_chip = node == 0
    is_source = jnp.logical_and(source_chip, core == 0)
    relays_w = core == 0
    relays_x = core == 1

    def send(src, dst, s_sem, r_sem, to):
        return pltpu.make_async_remote_copy(
            src_ref=src, dst_ref=dst, send_sem=s_sem, recv_sem=r_sem, device_id=to, device_id_type=MESH
        )

    def chunk(tree, step):
        at = TREE_BASE[tree] + step * CHUNK
        return pl.ds(pl.multiple_of(at, CHUNK), CHUNK)

    barrier = pltpu.get_barrier_semaphore()
    peers = [(inst, lax.rem(tp + k, N_TP)) for k in range(1, N_TP)]
    greeted = peers + z_others + [sibling, dims[2], right_other, left_other, across_other]
    for other in greeted:
        pl.semaphore_signal(barrier, inc=1, device_id=other, device_id_type=MESH)

    @pl.when(is_source)
    def _():
        for tree in range(3):

            def load(step, carry, tree=tree):
                rows = chunk(tree, step)
                pltpu.make_async_copy(w_in.at[0, rows], w.at[rows], recv_w.at[tree, step]).start()
                return carry

            lax.fori_loop(0, TREE_STEPS[tree], load, 0)

    foreign_cols = pl.ds(pl.multiple_of(((1 - y_hi) * 4 + x) * FEATS, FEATS), FEATS)
    own_cols = pl.ds(pl.multiple_of(tp * FEATS, FEATS), FEATS)
    wo_local = (
        pltpu.make_async_copy(wo_in.at[:, foreign_cols], wo.at[0, :, pl.ds(0, FEATS)], loc_wo.at[0]),
        pltpu.make_async_copy(wo_in.at[:, own_cols], wo.at[0, :, pl.ds(FEATS, FEATS)], loc_wo.at[1]),
    )
    for copy in wo_local:
        copy.start()

    eye = (
        lax.broadcasted_iota(jnp.int32, (128, 128), 0) == lax.broadcasted_iota(jnp.int32, (128, 128), 1)
    ).astype(F32)
    sums[tp] = jnp.zeros((8, 128), F32)
    gain_row = gain[pl.ds(pl.multiple_of(tp * FEATS, FEATS), FEATS)].reshape(1, FEATS)
    for g in range(4):
        wide = hidden[pl.ds(g * 128, 128), :].astype(F32)
        xs[0, pl.ds(g * 128, 128), :] = (wide * gain_row).astype(BF16)
        column = jnp.sum(wide * wide, axis=1, keepdims=True)
        sums[tp, pl.ds(g, 1), :] = jnp.sum(column * eye, axis=0, keepdims=True)

    pl.semaphore_wait(barrier, len(greeted))

    def piece(slot, p):
        return xs.at[slot, pl.ds(p * PIECE, PIECE)]

    def landed(block, p):
        return xl.at[block, pl.ds(p * PIECE, PIECE)]

    def send_piece(src, dst, sem, r_sem, to):
        send(src, dst, send_x.at[sem], r_sem, to).start()

    def wait_piece(slot, p):
        pltpu.make_async_copy(piece(slot, p), piece(slot, p), recv_x.at[slot, p]).wait()

    def wait_landed(block, p):
        pltpu.make_async_copy(landed(block, p), landed(block, p), recv_l.at[block, p]).wait()

    def to_final(src, slot, p, sem, to):
        send_piece(src, piece(slot, p), sem, recv_x.at[slot, p], to)

    def to_relay(src, block, p, sem, to):
        send_piece(src, landed(block, p), sem, recv_l.at[block, p], to)

    def cross(p):
        to_final(piece(0, p), 4, p, 2, opposite)
        to_relay(landed(3, p), 1, p, 2, opposite)

    @pl.when(relays_w)
    def _():
        for p in range(N_PIECES):
            to_relay(piece(0, p), 3, p, 2, sibling)

    @pl.when(relays_x)
    def _():
        for p in range(N_PIECES):
            to_final(piece(0, p), 2, p, 0, right)
            to_final(piece(0, p), 1, p, 1, left)
            wait_landed(3, p)
            if p % 2 == 0:
                to_relay(landed(3, p), 0, p, 0, right)
                to_final(landed(3, p), 1, p, 1, left_other)
            else:
                to_final(landed(3, p), 2, p, 0, right_other)
                to_relay(landed(3, p), 0, p, 1, left)
            if p in Y_FIRST:
                cross(p)

    for other in peers:
        send(sums.at[tp], sums.at[tp], send_s, recv_s.at[tp], other).start()

    def wo_block(quarter):
        return wo.at[pl.ds(1, 3), pl.ds(pl.multiple_of(lax.rem(z + quarter, 4) * 128, 128), 128), :]

    wo_targets = ((2, right_other, 1), (1, left_other, 3), (3, across_other, 2))

    def wo_sends(turn):
        rows = pl.ds(pl.multiple_of(lax.rem(z + 2 * turn, 4) * 128, 128), 128)
        for slot, to, shift in wo_targets:
            x_to = lax.rem(x + shift, 4)
            for part, y_part in ((0, 1 - y_hi), (1, y_hi)):
                cols = pl.ds(pl.multiple_of((y_part * 4 + x_to) * FEATS, FEATS), FEATS)
                send(
                    wo_in.at[rows, cols],
                    wo.at[slot, rows, pl.ds(part * FEATS, FEATS)],
                    send_wx.at[turn, slot - 1, part],
                    recv_wx.at[turn, slot - 1, part],
                    to,
                ).start()

    sends_tree = [
        [((MASKS[tree][dim] >> node) & 1) == 1 for dim in range(3)] for tree in range(3)
    ]

    def weight_tree(tree, step):
        rows = chunk(tree, step)
        pltpu.make_async_copy(w.at[rows], w.at[rows], recv_w.at[tree, step]).wait()
        for dim in range(3):
            if MASKS[tree][dim]:

                @pl.when(sends_tree[tree][dim])
                def _(dim=dim):
                    send(w.at[rows], w.at[rows], send_w.at[dim], recv_w.at[tree, step], dims[dim]).start()

        @pl.when(is_source)
        def _():
            turn = lax.rem(step, AHEAD)

            @pl.when(step >= AHEAD)
            def _():
                pltpu.make_async_copy(w.at[rows], w.at[rows], send_r.at[tree, turn]).wait()

            send(w.at[rows], w.at[rows], send_r.at[tree, turn], recv_w.at[tree, step], dims[tree]).start()

        send(w.at[rows], w.at[rows], send_sib, recv_w.at[tree, step], sibling).start()

    def wo_arrived(turn):
        rows = pl.ds(pl.multiple_of(lax.rem(z + 2 * turn, 4) * 128, 128), 128)
        for slot in range(3):
            for part in range(2):
                dst = wo.at[slot + 1, rows, pl.ds(part * FEATS, FEATS)]
                pltpu.make_async_copy(dst, dst, recv_wx.at[turn, slot, part]).wait()

    def wo_to_sibling(quarter):
        block = wo_block(quarter)
        send(block, block, send_ws.at[quarter], recv_ws.at[quarter], sibling).start()

    def wo_spread():
        wo_arrived(0)
        block = wo_block(0)
        for k, to in ((0, z_others[0]), (1, z_others[2])):
            send(block, block, send_wz.at[k], recv_wz.at[k], to).start()
        wo_to_sibling(0)

    def wo_pass(k):
        quarter = 3 - 2 * k
        block = wo_block(quarter)
        pltpu.make_async_copy(block, block, recv_wz.at[k]).wait()
        wo_to_sibling(quarter)

    def weight_steps():
        def slot_of(slot, carry):
            for tree in range(3):
                step = slot - LAG * ((DEPTHS[tree] >> (3 * node)) & 7)

                @pl.when(jnp.logical_and(step >= 0, step < TREE_STEPS[tree]))
                def _(tree=tree, step=step):
                    weight_tree(tree, step)

            return carry

        lax.fori_loop(0, N_SLOTS, slot_of, 0)

    def relay_ring(h, e):
        p = 2 * e
        wait_piece(4 * h + 2, p)
        to_final(piece(4 * h + 2, p), 4 * h + 3, p, 0, right)
        wait_landed(2 * h, p)
        to_final(landed(2 * h, p), 4 * h + 3, p, 0, right_other)
        to_final(landed(2 * h, p), 4 * h + 2, p, 3, sibling)
        p = 2 * e + 1
        wait_piece(4 * h + 1, p)
        to_final(piece(4 * h + 1, p), 4 * h + 3, p, 1, left)
        wait_landed(2 * h, p)
        to_final(landed(2 * h, p), 4 * h + 3, p, 1, left_other)
        to_final(landed(2 * h, p), 4 * h + 1, p, 3, sibling)

    def relay_opposite(p):
        wait_piece(4, p)
        to_final(piece(4, p), 6, p, 0, right)
        to_final(piece(4, p), 5, p, 1, left)
        wait_landed(1, p)
        if p % 2 == 0:
            to_relay(landed(1, p), 2, p, 0, right)
            to_final(landed(1, p), 5, p, 1, left_other)
        else:
            to_final(landed(1, p), 6, p, 0, right_other)
            to_relay(landed(1, p), 2, p, 1, left)
        to_final(landed(1, p), 4, p, 3, sibling)

    length = [lengths[0, k] for k in range(3)]
    begins = [length[0], length[0] + length[1], length[0] + length[1] + length[2]]

    def start_of(row):
        start = jnp.zeros_like(row)
        for begin in begins:
            start = jnp.where(row >= begin, begin, start)
        return start

    def fill_tables():
        cosine[...], sine[...] = rope_tables(start_of, ROWS)

    @pl.when(relays_w)
    def _():
        weight_steps()
        wo_spread()
        fill_tables()

    @pl.when(relays_x)
    def _():
        fill_tables()
        relay_ring(0, 0)
        relay_ring(0, 1)
        wo_sends(0)
        relay_opposite(0)
        relay_opposite(1)
        relay_ring(1, 0)
        for p in range(N_PIECES):
            if p not in Y_FIRST:
                cross(p)
        relay_opposite(2)
        relay_opposite(3)
        relay_ring(1, 1)
        wo_sends(1)

    @pl.when(relays_x)
    def _():
        for tree in range(3):

            def passed(step, carry, tree=tree):
                rows = chunk(tree, step)
                pltpu.make_async_copy(w.at[rows], w.at[rows], recv_w.at[tree, step]).wait()
                return carry

            lax.fori_loop(0, TREE_STEPS[tree], passed, 0)

    acc[...] = jnp.zeros_like(acc)

    def block_dot(slot, carry):
        turn = lax.rem(slot, 4)
        h = slot // 4

        for p in range(N_PIECES):
            relayed = (turn == 0) | ((turn == 2) & (p % 2 == 0)) | ((turn == 1) & (p % 2 == 1))
            seen = (slot == 0) | (relays_x & relayed)

            @pl.when(jnp.logical_not(seen))
            def _(p=p):
                wait_piece(slot, p)

        shift = jnp.where(turn == 2, 3, jnp.where(turn == 3, 2, turn))
        owner = lax.rem(y_hi + h, 2) * 4 + lax.rem(x + shift, 4)
        base = pl.multiple_of(owner * FEATS, FEATS)
        for n in range(3):
            cols = pl.ds(n * 256, 256)
            acc[:, cols] += jnp.dot(
                xs[slot], w[pl.ds(base, FEATS), cols], preferred_element_type=F32
            )
        return carry

    lax.fori_loop(0, 8, block_dot, 0)

    for k in range(1, N_TP):
        sender = lax.rem(tp + k, N_TP)
        pltpu.make_async_copy(sums.at[sender], sums.at[sender], recv_s.at[sender]).wait()
    total = sums[0]
    for t in range(1, N_TP):
        total = total + sums[t]
    factor = lax.rsqrt(total * (1.0 / D) + EPSILON)
    for g in range(4):
        inv[pl.ds(g * 128, 128), :] = jnp.sum(factor[g : g + 1, :] * eye, axis=1, keepdims=True) * jnp.ones(
            (1, 128), F32
        )

    def turned(value, rows):
        return value * cosine[rows, :] + pltpu.roll(value, HD // 2, axis=1) * sine[rows, :]

    def split(g, carry):
        rows = pl.ds(pl.multiple_of(g * 128, 128), 128)
        scale = inv[rows, :]
        for head in range(HEADS):
            qb[head, rows, :] = turned(acc[rows, pl.ds(head * HD, HD)] * scale, rows).astype(BF16)
        kb[rows, :] = turned(acc[rows, pl.ds(ATT_COLS, HD)] * scale, rows).astype(BF16)
        vb[rows, :] = (acc[rows, pl.ds(ATT_COLS + HD, HD)] * scale).astype(BF16)
        return carry

    lax.fori_loop(0, 4, split, 0)

    def att_rows(slot, q):
        return att.at[slot, pl.ds(q * TQ, TQ)]

    def att_half(slot, q, half):
        return att.at[slot, pl.ds(q * TQ + half * (TQ // 2), TQ // 2)]

    for q in range(N_Q):
        low = max(0, q * TQ - LONGEST)
        high = (q + 1) * TQ
        row = lax.broadcasted_iota(jnp.int32, (TQ, high - low), 0) + q * TQ
        key = lax.broadcasted_iota(jnp.int32, (TQ, high - low), 1) + low
        allowed = (key <= row) & (key >= start_of(row))
        for head in range(HEADS):
            scores = lax.dot_general(
                qb[head, pl.ds(q * TQ, TQ), :],
                kb[pl.ds(low, high - low), :],
                (((1,), (1,)), ((), ())),
                preferred_element_type=F32,
            ) * (1.0 / math.sqrt(HD))
            scores = jnp.where(allowed, scores, -1e30)
            largest = jnp.max(scores, axis=1, keepdims=True)
            weights = jnp.exp(jnp.where(allowed, scores - largest, -1e30))
            denominator = jnp.sum(weights, axis=1, keepdims=True)
            mixed = jnp.dot(weights.astype(BF16), vb[pl.ds(low, high - low), :], preferred_element_type=F32)
            att[0, pl.ds(q * TQ, TQ), pl.ds(head * HD, HD)] = (mixed / denominator).astype(BF16)
        send(att_rows(0, q), att_rows(2, q), send_a.at[0], recv_a.at[1, q], right).start()
        send(att_rows(0, q), att_rows(1, q), send_a.at[1], recv_a.at[0, q], left).start()

        @pl.when(relays_w)
        def _(q=q):
            if q in (1, 2):
                wo_pass(q - 1)
            elif q == 3:
                wo_arrived(1)
                wo_to_sibling(2)

    for copy in wo_local:
        copy.wait()

    @pl.when(relays_x)
    def _():
        for quarter in range(4):
            block = wo_block(quarter)
            pltpu.make_async_copy(block, block, recv_ws.at[quarter]).wait()

    def relay_att(q):
        pltpu.make_async_copy(att_rows(2, q), att_rows(2, q), recv_a.at[1, q]).wait()
        send(att_half(2, q, 0), att_half(3, q, 0), send_a.at[0], recv_a.at[2, q], right).start()
        pltpu.make_async_copy(att_rows(1, q), att_rows(1, q), recv_a.at[0, q]).wait()
        send(att_half(1, q, 1), att_half(3, q, 1), send_a.at[1], recv_a.at[3, q], left).start()

    def tile(q, cols):
        total = jnp.dot(att[0, pl.ds(q * TQ, TQ), :], wo[0, :, cols], preferred_element_type=F32)
        for slot in range(1, 4):
            total += jnp.dot(att[slot, pl.ds(q * TQ, TQ), :], wo[slot, :, cols], preferred_element_type=F32)
        return total

    def foreign_part(q):
        for half in range(2):
            pltpu.make_async_copy(att_half(3, q, half), att_half(3, q, half), recv_a.at[2 + half, q]).wait()

        def foreign(n, carry):
            cols = pl.ds(pl.multiple_of(n * 256, 256), 256)
            pf[pl.ds(q * TQ, TQ), cols] = tile(q, cols).astype(BF16)
            return carry

        lax.fori_loop(0, 4, foreign, 0)
        rows = pl.ds(q * TQ, TQ)
        send(pf.at[rows], rb.at[rows], send_y, recv_y.at[q], opposite).start()

    def own_part(q):
        def mine(n, carry):
            cols = pl.ds(pl.multiple_of(n * 256, 256), 256)
            own[pl.ds(q * TQ, TQ), cols] = tile(q, pl.ds(pl.multiple_of(FEATS + n * 256, 256), 256))
            return carry

        lax.fori_loop(0, 4, mine, 0)

    relay_att(0)
    for q in range(N_Q):
        if q + 1 < N_Q:
            relay_att(q + 1)
        foreign_part(q)
    for q in range(N_Q):
        own_part(q)
    for q in range(N_Q):
        rows = pl.ds(q * TQ, TQ)
        pltpu.make_async_copy(rb.at[rows], rb.at[rows], recv_y.at[q]).wait()
        out[rows, :] = (own[rows, :] + rb[rows, :].astype(F32)).astype(BF16)

    def sent(ref, sem):
        pltpu.make_async_copy(ref, ref, sem).wait()

    @pl.when(relays_w)
    def _():
        for tree in range(3):
            for dim in range(3):
                if MASKS[tree][dim]:

                    @pl.when(sends_tree[tree][dim])
                    def _(tree=tree, dim=dim):
                        sent(w.at[pl.ds(0, TREE_STEPS[tree] * CHUNK)], send_w.at[dim])

        @pl.when(is_source)
        def _():
            for tree in range(3):
                for turn in range(AHEAD):
                    sent(w.at[pl.ds(0, CHUNK)], send_r.at[tree, turn])

        sent(w, send_sib)
        sent(xs.at[0], send_x.at[2])
        for k in range(2):
            sent(wo_block(0), send_wz.at[k])
        for quarter in range(4):
            sent(wo_block(0), send_ws.at[quarter])

    @pl.when(relays_x)
    def _():
        for side in range(2):
            sent(xs.at[pl.ds(0, 6)], send_x.at[side])
        sent(xs.at[pl.ds(0, 2)], send_x.at[2])
        sent(xs.at[pl.ds(0, 3)], send_x.at[3])
        for turn in range(2):
            for slot in range(3):
                for part in range(2):
                    sent(wo.at[0, pl.ds(0, 128), pl.ds(0, FEATS)], send_wx.at[turn, slot, part])

    sent(sums.at[pl.ds(0, 7)], send_s)
    for side in range(2):
        sent(att.at[0], send_a.at[side])
        sent(att.at[0, pl.ds(0, ROWS // 2)], send_a.at[side])
    sent(pf, send_y)


def local(hidden_rows, lengths, attn_gain, w_joined, w_out):
    dma = pltpu.SemaphoreType.DMA
    vmem = pl.BlockSpec(memory_space=pltpu.VMEM)
    anywhere = pl.BlockSpec(memory_space=pl.ANY)
    return pl.pallas_call(
        body,
        out_shape=jax.ShapeDtypeStruct((ROWS, FEATS), BF16),
        in_specs=[vmem, pl.BlockSpec(memory_space=pltpu.SMEM), vmem, anywhere, anywhere],
        out_specs=vmem,
        scratch_shapes=[
            pltpu.VMEM((D, COLS), BF16),
            pltpu.VMEM((8, ROWS, FEATS), BF16),
            pltpu.VMEM((4, ROWS, FEATS), BF16),
            pltpu.VMEM((4, ATT_COLS, 2 * FEATS), BF16),
            pltpu.VMEM((ROWS, COLS), F32),
            pltpu.VMEM((4, ROWS, ATT_COLS), BF16),
            pltpu.VMEM((ROWS, FEATS), BF16),
            pltpu.VMEM((ROWS, FEATS), BF16),
            pltpu.VMEM((ROWS, FEATS), F32),
            pltpu.VMEM((N_TP, 8, 128), F32),
            pltpu.VMEM((ROWS, 128), F32),
            pltpu.VMEM((ROWS, HD), F32),
            pltpu.VMEM((ROWS, HD), F32),
            pltpu.VMEM((HEADS, ROWS, HD), BF16),
            pltpu.VMEM((ROWS, HD), BF16),
            pltpu.VMEM((ROWS, HD), BF16),
            dma((3, max(TREE_STEPS))),
            dma((3,)),
            dma((3, AHEAD)),
            dma,
            dma((8, N_PIECES)),
            dma((4, N_PIECES)),
            dma((4,)),
            dma((N_TP,)),
            dma,
            dma((2, 3, 2)),
            dma((2, 3, 2)),
            dma((2,)),
            dma((2,)),
            dma((4,)),
            dma((4,)),
            dma((2,)),
            dma((4, N_Q)),
            dma((2,)),
            dma((N_Q,)),
            dma,
        ],
        compiler_params=pltpu.CompilerParams(
            collective_id=0, has_side_effects=True, vmem_limit_bytes=56 * 1024 * 1024
        ),
    )(hidden_rows, lengths, attn_gain, w_joined, w_out)


def solution(mesh):
    return jax.shard_map(
        local,
        mesh=mesh,
        in_specs=(P("inst", "tp"), P("inst", None), P(), P("inst", None, "tp"), P("tp", None)),
        out_specs=P("inst", "tp"),
        check_vma=False,
    )
```

```python
import functools
import math

import jax
import jax.numpy as jnp
from jax import lax
from jax.experimental import pallas as pl
from jax.experimental.pallas import tpu as pltpu
from jax.sharding import PartitionSpec as P

MESH = pl.DeviceIdType.MESH
F32 = jnp.float32
BF16 = jnp.bfloat16

KVHEADS = 8
HD = 128
QHEADS = 32
ROWS = 512
D = 8192
N_TP = 8
FEATS = D // N_TP
COLS = 768
HEADS = QHEADS // N_TP
ATT_COLS = HEADS * HD
LONGEST = 256

EPSILON = 1e-05
ROPE_BASE = 500000.0
ROPE_FACTOR = 8.0
LOW_FACTOR = 1.0
HIGH_FACTOR = 4.0
OLD_CONTEXT = 8192.0

CHUNK = 64
TREE_STEPS = (44, 44, 40)
TREE_BASE = (0, 2816, 5632)
GRAY = (0, 1, 3, 2)
LAG = 4
AHEAD = 4
N_SLOTS = max(TREE_STEPS) + 4 * LAG

Y_FIRST = (0, 1, 2)
PIECE = 128
N_PIECES = ROWS // PIECE
TQ = 128
N_Q = ROWS // TQ


def tree_masks():
    masks = [[0] * 3 for _ in range(3)]
    depths = [0] * 3
    node_of = {}
    for y_lo in range(2):
        for z in range(4):
            node_of[y_lo * 4 + GRAY[z]] = y_lo * 4 + z
    first_edges = [(0, 0), (1, 1), (1, 2), (3, 2), (3, 0), (5, 0), (7, 0)]
    for tree in range(3):
        depth = {0: 0}
        for code, dim in first_edges:
            depth[code ^ (1 << dim)] = depth[code] + 1
            turned = ((code << tree) | (code >> (3 - tree))) & 7
            if code:
                masks[tree][(dim + tree) % 3] |= 1 << node_of[turned]
        for code, far in depth.items():
            turned = ((code << tree) | (code >> (3 - tree))) & 7
            depths[tree] |= far << (3 * node_of[turned])
    return masks, depths


MASKS, DEPTHS = tree_masks()


def rope_tables(start_of, rows):
    lane = lax.broadcasted_iota(jnp.int32, (1, HD), 1)
    index = lax.rem(lane, HD // 2).astype(F32)
    base = jnp.exp(index * (-2.0 * math.log(ROPE_BASE) / HD))
    wavelength = 2.0 * math.pi / base
    blending = (OLD_CONTEXT / wavelength - LOW_FACTOR) / (HIGH_FACTOR - LOW_FACTOR)
    blended = (1.0 - blending) * base / ROPE_FACTOR + blending * base
    slowed = jnp.where(wavelength > OLD_CONTEXT / LOW_FACTOR, base / ROPE_FACTOR, blended)
    frequency = jnp.where(wavelength < OLD_CONTEXT / HIGH_FACTOR, base, slowed)
    row = lax.broadcasted_iota(jnp.int32, (rows, HD), 0)
    angles = (row - start_of(row)).astype(F32) * frequency
    sine = jnp.sin(angles)
    return jnp.cos(angles), jnp.where(lane < HD // 2, -sine, sine)


def body(
    hidden, lengths, gain, w_in, wo_in, out,
    w, xs, xl, wo, acc, att, pf, rb, own, sums, inv, cosine, sine, qb, kb, vb,
    recv_w, send_w, send_r, send_sib, recv_x, recv_l, send_x, recv_s, send_s,
    recv_wx, send_wx, recv_wz, send_wz, recv_ws, send_ws, loc_wo,
    recv_a, send_a, recv_y, send_y,
):
    inst = lax.axis_index("inst")
    tp = lax.axis_index("tp")
    core = lax.rem(inst, 2)
    z = lax.rem(inst // 2, 4)
    y_lo = inst // 8
    x = lax.rem(tp, 4)
    y_hi = tp // 4

    def inst_of(y_lo_, z_, core_):
        return (y_lo_ * 4 + z_) * 2 + core_

    tp_right = y_hi * 4 + lax.rem(x + 1, 4)
    tp_left = y_hi * 4 + lax.rem(x + 3, 4)
    right = (inst, tp_right)
    left = (inst, tp_left)
    tp_opposite = (1 - y_hi) * 4 + x
    opposite = (inst, tp_opposite)
    other_inst = inst_of(y_lo, z, 1 - core)
    sibling = (other_inst, tp)
    right_other = (other_inst, tp_right)
    left_other = (other_inst, tp_left)
    across_other = (other_inst, y_hi * 4 + lax.rem(x + 2, 4))
    dims = (
        (inst_of(y_lo, z + 1 - 2 * lax.rem(z, 2), core), tp),
        (inst_of(y_lo, 3 - z, core), tp),
        (inst_of(1 - y_lo, z, core), tp),
    )
    z_others = [(inst_of(y_lo, lax.rem(z + k, 4), core), tp) for k in (1, 2, 3)]
    node = y_lo * 4 + z
    source_chip = node == 0
    is_source = jnp.logical_and(source_chip, core == 0)
    relays_w = core == 0
    relays_x = core == 1

    def send(src, dst, s_sem, r_sem, to):
        return pltpu.make_async_remote_copy(
            src_ref=src, dst_ref=dst, send_sem=s_sem, recv_sem=r_sem, device_id=to, device_id_type=MESH
        )

    def chunk(tree, step):
        at = TREE_BASE[tree] + step * CHUNK
        return pl.ds(pl.multiple_of(at, CHUNK), CHUNK)

    barrier = pltpu.get_barrier_semaphore()
    peers = [(inst, lax.rem(tp + k, N_TP)) for k in range(1, N_TP)]
    greeted = peers + z_others + [sibling, dims[2], right_other, left_other, across_other]
    for other in greeted:
        pl.semaphore_signal(barrier, inc=1, device_id=other, device_id_type=MESH)

    @pl.when(is_source)
    def _():
        for tree in range(3):

            def load(step, carry, tree=tree):
                rows = chunk(tree, step)
                pltpu.make_async_copy(w_in.at[0, rows], w.at[rows], recv_w.at[tree, step]).start()
                return carry

            lax.fori_loop(0, TREE_STEPS[tree], load, 0)

    foreign_cols = pl.ds(pl.multiple_of(((1 - y_hi) * 4 + x) * FEATS, FEATS), FEATS)
    own_cols = pl.ds(pl.multiple_of(tp * FEATS, FEATS), FEATS)
    wo_local = (
        pltpu.make_async_copy(wo_in.at[:, foreign_cols], wo.at[0, :, pl.ds(0, FEATS)], loc_wo.at[0]),
        pltpu.make_async_copy(wo_in.at[:, own_cols], wo.at[0, :, pl.ds(FEATS, FEATS)], loc_wo.at[1]),
    )
    for copy in wo_local:
        copy.start()

    eye = (
        lax.broadcasted_iota(jnp.int32, (128, 128), 0) == lax.broadcasted_iota(jnp.int32, (128, 128), 1)
    ).astype(F32)
    sums[tp] = jnp.zeros((8, 128), F32)
    gain_row = gain[pl.ds(pl.multiple_of(tp * FEATS, FEATS), FEATS)].reshape(1, FEATS)
    for g in range(4):
        wide = hidden[pl.ds(g * 128, 128), :].astype(F32)
        xs[0, pl.ds(g * 128, 128), :] = (wide * gain_row).astype(BF16)
        column = jnp.sum(wide * wide, axis=1, keepdims=True)
        sums[tp, pl.ds(g, 1), :] = jnp.sum(column * eye, axis=0, keepdims=True)

    pl.semaphore_wait(barrier, len(greeted))

    def piece(slot, p):
        return xs.at[slot, pl.ds(p * PIECE, PIECE)]

    def landed(block, p):
        return xl.at[block, pl.ds(p * PIECE, PIECE)]

    def send_piece(src, dst, sem, r_sem, to):
        send(src, dst, send_x.at[sem], r_sem, to).start()

    def wait_piece(slot, p):
        pltpu.make_async_copy(piece(slot, p), piece(slot, p), recv_x.at[slot, p]).wait()

    def wait_landed(block, p):
        pltpu.make_async_copy(landed(block, p), landed(block, p), recv_l.at[block, p]).wait()

    def to_final(src, slot, p, sem, to):
        send_piece(src, piece(slot, p), sem, recv_x.at[slot, p], to)

    def to_relay(src, block, p, sem, to):
        send_piece(src, landed(block, p), sem, recv_l.at[block, p], to)

    def cross(p):
        to_final(piece(0, p), 4, p, 2, opposite)
        to_relay(landed(3, p), 1, p, 2, opposite)

    @pl.when(relays_w)
    def _():
        for p in range(N_PIECES):
            to_relay(piece(0, p), 3, p, 2, sibling)

    @pl.when(relays_x)
    def _():
        for p in range(N_PIECES):
            to_final(piece(0, p), 2, p, 0, right)
            to_final(piece(0, p), 1, p, 1, left)
            wait_landed(3, p)
            if p % 2 == 0:
                to_relay(landed(3, p), 0, p, 0, right)
                to_final(landed(3, p), 1, p, 1, left_other)
            else:
                to_final(landed(3, p), 2, p, 0, right_other)
                to_relay(landed(3, p), 0, p, 1, left)
            if p in Y_FIRST:
                cross(p)

    for other in peers:
        send(sums.at[tp], sums.at[tp], send_s, recv_s.at[tp], other).start()

    def wo_block(quarter):
        return wo.at[pl.ds(1, 3), pl.ds(pl.multiple_of(lax.rem(z + quarter, 4) * 128, 128), 128), :]

    wo_targets = ((2, right_other, 1), (1, left_other, 3), (3, across_other, 2))

    def wo_sends(turn):
        rows = pl.ds(pl.multiple_of(lax.rem(z + 2 * turn, 4) * 128, 128), 128)
        for slot, to, shift in wo_targets:
            x_to = lax.rem(x + shift, 4)
            for part, y_part in ((0, 1 - y_hi), (1, y_hi)):
                cols = pl.ds(pl.multiple_of((y_part * 4 + x_to) * FEATS, FEATS), FEATS)
                send(
                    wo_in.at[rows, cols],
                    wo.at[slot, rows, pl.ds(part * FEATS, FEATS)],
                    send_wx.at[turn, slot - 1, part],
                    recv_wx.at[turn, slot - 1, part],
                    to,
                ).start()

    sends_tree = [
        [((MASKS[tree][dim] >> node) & 1) == 1 for dim in range(3)] for tree in range(3)
    ]

    def weight_tree(tree, step):
        rows = chunk(tree, step)
        pltpu.make_async_copy(w.at[rows], w.at[rows], recv_w.at[tree, step]).wait()
        for dim in range(3):
            if MASKS[tree][dim]:

                @pl.when(sends_tree[tree][dim])
                def _(dim=dim):
                    send(w.at[rows], w.at[rows], send_w.at[dim], recv_w.at[tree, step], dims[dim]).start()

        @pl.when(is_source)
        def _():
            turn = lax.rem(step, AHEAD)

            @pl.when(step >= AHEAD)
            def _():
                pltpu.make_async_copy(w.at[rows], w.at[rows], send_r.at[tree, turn]).wait()

            send(w.at[rows], w.at[rows], send_r.at[tree, turn], recv_w.at[tree, step], dims[tree]).start()

        send(w.at[rows], w.at[rows], send_sib, recv_w.at[tree, step], sibling).start()

    def wo_arrived(turn):
        rows = pl.ds(pl.multiple_of(lax.rem(z + 2 * turn, 4) * 128, 128), 128)
        for slot in range(3):
            for part in range(2):
                dst = wo.at[slot + 1, rows, pl.ds(part * FEATS, FEATS)]
                pltpu.make_async_copy(dst, dst, recv_wx.at[turn, slot, part]).wait()

    def wo_to_sibling(quarter):
        block = wo_block(quarter)
        send(block, block, send_ws.at[quarter], recv_ws.at[quarter], sibling).start()

    def wo_spread():
        wo_arrived(0)
        block = wo_block(0)
        for k, to in ((0, z_others[0]), (1, z_others[2])):
            send(block, block, send_wz.at[k], recv_wz.at[k], to).start()
        wo_to_sibling(0)

    def wo_pass(k):
        quarter = 3 - 2 * k
        block = wo_block(quarter)
        pltpu.make_async_copy(block, block, recv_wz.at[k]).wait()
        wo_to_sibling(quarter)

    def weight_steps():
        def slot_of(slot, carry):
            for tree in range(3):
                step = slot - LAG * ((DEPTHS[tree] >> (3 * node)) & 7)

                @pl.when(jnp.logical_and(step >= 0, step < TREE_STEPS[tree]))
                def _(tree=tree, step=step):
                    weight_tree(tree, step)

            return carry

        lax.fori_loop(0, N_SLOTS, slot_of, 0)

    def relay_ring(h, e):
        p = 2 * e
        wait_piece(4 * h + 2, p)
        to_final(piece(4 * h + 2, p), 4 * h + 3, p, 0, right)
        wait_landed(2 * h, p)
        to_final(landed(2 * h, p), 4 * h + 3, p, 0, right_other)
        to_final(landed(2 * h, p), 4 * h + 2, p, 3, sibling)
        p = 2 * e + 1
        wait_piece(4 * h + 1, p)
        to_final(piece(4 * h + 1, p), 4 * h + 3, p, 1, left)
        wait_landed(2 * h, p)
        to_final(landed(2 * h, p), 4 * h + 3, p, 1, left_other)
        to_final(landed(2 * h, p), 4 * h + 1, p, 3, sibling)

    def relay_opposite(p):
        wait_piece(4, p)
        to_final(piece(4, p), 6, p, 0, right)
        to_final(piece(4, p), 5, p, 1, left)
        wait_landed(1, p)
        if p % 2 == 0:
            to_relay(landed(1, p), 2, p, 0, right)
            to_final(landed(1, p), 5, p, 1, left_other)
        else:
            to_final(landed(1, p), 6, p, 0, right_other)
            to_relay(landed(1, p), 2, p, 1, left)
        to_final(landed(1, p), 4, p, 3, sibling)

    length = [lengths[0, k] for k in range(3)]
    begins = [length[0], length[0] + length[1], length[0] + length[1] + length[2]]

    def start_of(row):
        start = jnp.zeros_like(row)
        for begin in begins:
            start = jnp.where(row >= begin, begin, start)
        return start

    def fill_tables():
        cosine[...], sine[...] = rope_tables(start_of, ROWS)

    @pl.when(relays_w)
    def _():
        weight_steps()
        wo_spread()
        fill_tables()

    @pl.when(relays_x)
    def _():
        fill_tables()
        relay_ring(0, 0)
        relay_ring(0, 1)
        wo_sends(0)
        relay_opposite(0)
        relay_opposite(1)
        relay_ring(1, 0)
        for p in range(N_PIECES):
            if p not in Y_FIRST:
                cross(p)
        relay_opposite(2)
        relay_opposite(3)
        relay_ring(1, 1)
        wo_sends(1)

    @pl.when(relays_x)
    def _():
        for tree in range(3):

            def passed(step, carry, tree=tree):
                rows = chunk(tree, step)
                pltpu.make_async_copy(w.at[rows], w.at[rows], recv_w.at[tree, step]).wait()
                return carry

            lax.fori_loop(0, TREE_STEPS[tree], passed, 0)

    acc[...] = jnp.zeros_like(acc)

    def block_dot(slot, carry):
        turn = lax.rem(slot, 4)
        h = slot // 4

        for p in range(N_PIECES):
            relayed = (turn == 0) | ((turn == 2) & (p % 2 == 0)) | ((turn == 1) & (p % 2 == 1))
            seen = (slot == 0) | (relays_x & relayed)

            @pl.when(jnp.logical_not(seen))
            def _(p=p):
                wait_piece(slot, p)

        shift = jnp.where(turn == 2, 3, jnp.where(turn == 3, 2, turn))
        owner = lax.rem(y_hi + h, 2) * 4 + lax.rem(x + shift, 4)
        base = pl.multiple_of(owner * FEATS, FEATS)
        for n in range(3):
            cols = pl.ds(n * 256, 256)
            acc[:, cols] += jnp.dot(
                xs[slot], w[pl.ds(base, FEATS), cols], preferred_element_type=F32
            )
        return carry

    lax.fori_loop(0, 8, block_dot, 0)

    for k in range(1, N_TP):
        sender = lax.rem(tp + k, N_TP)
        pltpu.make_async_copy(sums.at[sender], sums.at[sender], recv_s.at[sender]).wait()
    total = sums[0]
    for t in range(1, N_TP):
        total = total + sums[t]
    factor = lax.rsqrt(total * (1.0 / D) + EPSILON)
    for g in range(4):
        inv[pl.ds(g * 128, 128), :] = jnp.sum(factor[g : g + 1, :] * eye, axis=1, keepdims=True) * jnp.ones(
            (1, 128), F32
        )

    def turned(value, rows):
        return value * cosine[rows, :] + pltpu.roll(value, HD // 2, axis=1) * sine[rows, :]

    def split(g, carry):
        rows = pl.ds(pl.multiple_of(g * 128, 128), 128)
        scale = inv[rows, :]
        for head in range(HEADS):
            qb[head, rows, :] = turned(acc[rows, pl.ds(head * HD, HD)] * scale, rows).astype(BF16)
        kb[rows, :] = turned(acc[rows, pl.ds(ATT_COLS, HD)] * scale, rows).astype(BF16)
        vb[rows, :] = (acc[rows, pl.ds(ATT_COLS + HD, HD)] * scale).astype(BF16)
        return carry

    lax.fori_loop(0, 4, split, 0)

    def att_rows(slot, q):
        return att.at[slot, pl.ds(q * TQ, TQ)]

    def att_half(slot, q, half):
        return att.at[slot, pl.ds(q * TQ + half * (TQ // 2), TQ // 2)]

    for q in range(N_Q):
        low = max(0, q * TQ - LONGEST)
        high = (q + 1) * TQ
        row = lax.broadcasted_iota(jnp.int32, (TQ, high - low), 0) + q * TQ
        key = lax.broadcasted_iota(jnp.int32, (TQ, high - low), 1) + low
        allowed = (key <= row) & (key >= start_of(row))
        for head in range(HEADS):
            scores = lax.dot_general(
                qb[head, pl.ds(q * TQ, TQ), :],
                kb[pl.ds(low, high - low), :],
                (((1,), (1,)), ((), ())),
                preferred_element_type=F32,
            ) * (1.0 / math.sqrt(HD))
            scores = jnp.where(allowed, scores, -1e30)
            largest = jnp.max(scores, axis=1, keepdims=True)
            weights = jnp.exp(jnp.where(allowed, scores - largest, -1e30))
            denominator = jnp.sum(weights, axis=1, keepdims=True)
            mixed = jnp.dot(weights.astype(BF16), vb[pl.ds(low, high - low), :], preferred_element_type=F32)
            att[0, pl.ds(q * TQ, TQ), pl.ds(head * HD, HD)] = (mixed / denominator).astype(BF16)
        send(att_rows(0, q), att_rows(2, q), send_a.at[0], recv_a.at[1, q], right).start()
        send(att_rows(0, q), att_rows(1, q), send_a.at[1], recv_a.at[0, q], left).start()

        @pl.when(relays_w)
        def _(q=q):
            if q == 3:
                wo_pass(0)
                wo_pass(1)
                wo_arrived(1)
                wo_to_sibling(2)

    for copy in wo_local:
        copy.wait()

    @pl.when(relays_x)
    def _():
        for quarter in range(4):
            block = wo_block(quarter)
            pltpu.make_async_copy(block, block, recv_ws.at[quarter]).wait()

    def relay_att(q):
        pltpu.make_async_copy(att_rows(2, q), att_rows(2, q), recv_a.at[1, q]).wait()
        send(att_half(2, q, 0), att_half(3, q, 0), send_a.at[0], recv_a.at[2, q], right).start()
        pltpu.make_async_copy(att_rows(1, q), att_rows(1, q), recv_a.at[0, q]).wait()
        send(att_half(1, q, 1), att_half(3, q, 1), send_a.at[1], recv_a.at[3, q], left).start()

    def tile(q, cols):
        total = jnp.dot(att[0, pl.ds(q * TQ, TQ), :], wo[0, :, cols], preferred_element_type=F32)
        for slot in range(1, 4):
            total += jnp.dot(att[slot, pl.ds(q * TQ, TQ), :], wo[slot, :, cols], preferred_element_type=F32)
        return total

    def foreign_part(q):
        for half in range(2):
            pltpu.make_async_copy(att_half(3, q, half), att_half(3, q, half), recv_a.at[2 + half, q]).wait()

        def foreign(n, carry):
            cols = pl.ds(pl.multiple_of(n * 256, 256), 256)
            pf[pl.ds(q * TQ, TQ), cols] = tile(q, cols).astype(BF16)
            return carry

        lax.fori_loop(0, 4, foreign, 0)
        rows = pl.ds(q * TQ, TQ)
        send(pf.at[rows], rb.at[rows], send_y, recv_y.at[q], opposite).start()

    def own_part(q):
        def mine(n, carry):
            cols = pl.ds(pl.multiple_of(n * 256, 256), 256)
            own[pl.ds(q * TQ, TQ), cols] = tile(q, pl.ds(pl.multiple_of(FEATS + n * 256, 256), 256))
            return carry

        lax.fori_loop(0, 4, mine, 0)

    relay_att(0)
    for q in range(N_Q):
        if q + 1 < N_Q:
            relay_att(q + 1)
        foreign_part(q)
    for q in range(N_Q):
        own_part(q)
    for q in range(N_Q):
        rows = pl.ds(q * TQ, TQ)
        pltpu.make_async_copy(rb.at[rows], rb.at[rows], recv_y.at[q]).wait()
        out[rows, :] = (own[rows, :] + rb[rows, :].astype(F32)).astype(BF16)

    def sent(ref, sem):
        pltpu.make_async_copy(ref, ref, sem).wait()

    @pl.when(relays_w)
    def _():
        for tree in range(3):
            for dim in range(3):
                if MASKS[tree][dim]:

                    @pl.when(sends_tree[tree][dim])
                    def _(tree=tree, dim=dim):
                        sent(w.at[pl.ds(0, TREE_STEPS[tree] * CHUNK)], send_w.at[dim])

        @pl.when(is_source)
        def _():
            for tree in range(3):
                for turn in range(AHEAD):
                    sent(w.at[pl.ds(0, CHUNK)], send_r.at[tree, turn])

        sent(w, send_sib)
        sent(xs.at[0], send_x.at[2])
        for k in range(2):
            sent(wo_block(0), send_wz.at[k])
        for quarter in range(4):
            sent(wo_block(0), send_ws.at[quarter])

    @pl.when(relays_x)
    def _():
        for side in range(2):
            sent(xs.at[pl.ds(0, 6)], send_x.at[side])
        sent(xs.at[pl.ds(0, 2)], send_x.at[2])
        sent(xs.at[pl.ds(0, 3)], send_x.at[3])
        for turn in range(2):
            for slot in range(3):
                for part in range(2):
                    sent(wo.at[0, pl.ds(0, 128), pl.ds(0, FEATS)], send_wx.at[turn, slot, part])

    sent(sums.at[pl.ds(0, 7)], send_s)
    for side in range(2):
        sent(att.at[0], send_a.at[side])
        sent(att.at[0, pl.ds(0, ROWS // 2)], send_a.at[side])
    sent(pf, send_y)


def local(hidden_rows, lengths, attn_gain, w_joined, w_out):
    dma = pltpu.SemaphoreType.DMA
    vmem = pl.BlockSpec(memory_space=pltpu.VMEM)
    anywhere = pl.BlockSpec(memory_space=pl.ANY)
    return pl.pallas_call(
        body,
        out_shape=jax.ShapeDtypeStruct((ROWS, FEATS), BF16),
        in_specs=[vmem, pl.BlockSpec(memory_space=pltpu.SMEM), vmem, anywhere, anywhere],
        out_specs=vmem,
        scratch_shapes=[
            pltpu.VMEM((D, COLS), BF16),
            pltpu.VMEM((8, ROWS, FEATS), BF16),
            pltpu.VMEM((4, ROWS, FEATS), BF16),
            pltpu.VMEM((4, ATT_COLS, 2 * FEATS), BF16),
            pltpu.VMEM((ROWS, COLS), F32),
            pltpu.VMEM((4, ROWS, ATT_COLS), BF16),
            pltpu.VMEM((ROWS, FEATS), BF16),
            pltpu.VMEM((ROWS, FEATS), BF16),
            pltpu.VMEM((ROWS, FEATS), F32),
            pltpu.VMEM((N_TP, 8, 128), F32),
            pltpu.VMEM((ROWS, 128), F32),
            pltpu.VMEM((ROWS, HD), F32),
            pltpu.VMEM((ROWS, HD), F32),
            pltpu.VMEM((HEADS, ROWS, HD), BF16),
            pltpu.VMEM((ROWS, HD), BF16),
            pltpu.VMEM((ROWS, HD), BF16),
            dma((3, max(TREE_STEPS))),
            dma((3,)),
            dma((3, AHEAD)),
            dma,
            dma((8, N_PIECES)),
            dma((4, N_PIECES)),
            dma((4,)),
            dma((N_TP,)),
            dma,
            dma((2, 3, 2)),
            dma((2, 3, 2)),
            dma((2,)),
            dma((2,)),
            dma((4,)),
            dma((4,)),
            dma((2,)),
            dma((4, N_Q)),
            dma((2,)),
            dma((N_Q,)),
            dma,
        ],
        compiler_params=pltpu.CompilerParams(
            collective_id=0, has_side_effects=True, vmem_limit_bytes=56 * 1024 * 1024
        ),
    )(hidden_rows, lengths, attn_gain, w_joined, w_out)


def solution(mesh):
    return jax.shard_map(
        local,
        mesh=mesh,
        in_specs=(P("inst", "tp"), P("inst", None), P(), P("inst", None, "tp"), P("tp", None)),
        out_specs=P("inst", "tp"),
        check_vma=False,
    )
```

```python
import functools
import math

import jax
import jax.numpy as jnp
from jax import lax
from jax.experimental import pallas as pl
from jax.experimental.pallas import tpu as pltpu
from jax.sharding import PartitionSpec as P

MESH = pl.DeviceIdType.MESH
F32 = jnp.float32
BF16 = jnp.bfloat16

KVHEADS = 8
HD = 128
QHEADS = 32
ROWS = 512
D = 8192
N_TP = 8
FEATS = D // N_TP
COLS = 768
HEADS = QHEADS // N_TP
ATT_COLS = HEADS * HD
LONGEST = 256

EPSILON = 1e-05
ROPE_BASE = 500000.0
ROPE_FACTOR = 8.0
LOW_FACTOR = 1.0
HIGH_FACTOR = 4.0
OLD_CONTEXT = 8192.0

CHUNK = 64
TREE_STEPS = (44, 44, 40)
TREE_BASE = (0, 2816, 5632)
GRAY = (0, 1, 3, 2)
LAG = 4
AHEAD = 4
N_SLOTS = max(TREE_STEPS) + 4 * LAG

Y_FIRST = (0, 1, 2)
PIECE = 128
N_PIECES = ROWS // PIECE
TQ = 128
N_Q = ROWS // TQ


def tree_masks():
    masks = [[0] * 3 for _ in range(3)]
    depths = [0] * 3
    node_of = {}
    for y_lo in range(2):
        for z in range(4):
            node_of[y_lo * 4 + GRAY[z]] = y_lo * 4 + z
    first_edges = [(0, 0), (1, 1), (1, 2), (3, 2), (3, 0), (5, 0), (7, 0)]
    for tree in range(3):
        depth = {0: 0}
        for code, dim in first_edges:
            depth[code ^ (1 << dim)] = depth[code] + 1
            turned = ((code << tree) | (code >> (3 - tree))) & 7
            if code:
                masks[tree][(dim + tree) % 3] |= 1 << node_of[turned]
        for code, far in depth.items():
            turned = ((code << tree) | (code >> (3 - tree))) & 7
            depths[tree] |= far << (3 * node_of[turned])
    return masks, depths


MASKS, DEPTHS = tree_masks()


def rope_tables(start_of, rows):
    lane = lax.broadcasted_iota(jnp.int32, (1, HD), 1)
    index = lax.rem(lane, HD // 2).astype(F32)
    base = jnp.exp(index * (-2.0 * math.log(ROPE_BASE) / HD))
    wavelength = 2.0 * math.pi / base
    blending = (OLD_CONTEXT / wavelength - LOW_FACTOR) / (HIGH_FACTOR - LOW_FACTOR)
    blended = (1.0 - blending) * base / ROPE_FACTOR + blending * base
    slowed = jnp.where(wavelength > OLD_CONTEXT / LOW_FACTOR, base / ROPE_FACTOR, blended)
    frequency = jnp.where(wavelength < OLD_CONTEXT / HIGH_FACTOR, base, slowed)
    row = lax.broadcasted_iota(jnp.int32, (rows, HD), 0)
    angles = (row - start_of(row)).astype(F32) * frequency
    sine = jnp.sin(angles)
    return jnp.cos(angles), jnp.where(lane < HD // 2, -sine, sine)


def body(
    hidden, lengths, gain, w_in, wo_in, out,
    w, xs, xl, wo, acc, att, pf, rb, own, sums, inv, cosine, sine, qb, kb, vb,
    recv_w, send_w, send_r, send_sib, recv_x, recv_l, send_x, recv_s, send_s,
    recv_wx, send_wx, recv_wz, send_wz, recv_ws, send_ws, loc_wo,
    recv_a, send_a, recv_y, send_y,
):
    inst = lax.axis_index("inst")
    tp = lax.axis_index("tp")
    core = lax.rem(inst, 2)
    z = lax.rem(inst // 2, 4)
    y_lo = inst // 8
    x = lax.rem(tp, 4)
    y_hi = tp // 4

    def inst_of(y_lo_, z_, core_):
        return (y_lo_ * 4 + z_) * 2 + core_

    tp_right = y_hi * 4 + lax.rem(x + 1, 4)
    tp_left = y_hi * 4 + lax.rem(x + 3, 4)
    right = (inst, tp_right)
    left = (inst, tp_left)
    tp_opposite = (1 - y_hi) * 4 + x
    opposite = (inst, tp_opposite)
    other_inst = inst_of(y_lo, z, 1 - core)
    sibling = (other_inst, tp)
    right_other = (other_inst, tp_right)
    left_other = (other_inst, tp_left)
    across_other = (other_inst, y_hi * 4 + lax.rem(x + 2, 4))
    dims = (
        (inst_of(y_lo, z + 1 - 2 * lax.rem(z, 2), core), tp),
        (inst_of(y_lo, 3 - z, core), tp),
        (inst_of(1 - y_lo, z, core), tp),
    )
    z_others = [(inst_of(y_lo, lax.rem(z + k, 4), core), tp) for k in (1, 2, 3)]
    node = y_lo * 4 + z
    source_chip = node == 0
    is_source = jnp.logical_and(source_chip, core == 0)
    relays_w = core == 0
    relays_x = core == 1

    def send(src, dst, s_sem, r_sem, to):
        return pltpu.make_async_remote_copy(
            src_ref=src, dst_ref=dst, send_sem=s_sem, recv_sem=r_sem, device_id=to, device_id_type=MESH
        )

    def chunk(tree, step):
        at = TREE_BASE[tree] + step * CHUNK
        return pl.ds(pl.multiple_of(at, CHUNK), CHUNK)

    barrier = pltpu.get_barrier_semaphore()
    peers = [(inst, lax.rem(tp + k, N_TP)) for k in range(1, N_TP)]
    greeted = peers + z_others + [sibling, dims[2], right_other, left_other, across_other]
    for other in greeted:
        pl.semaphore_signal(barrier, inc=1, device_id=other, device_id_type=MESH)

    @pl.when(is_source)
    def _():
        for tree in range(3):

            def load(step, carry, tree=tree):
                rows = chunk(tree, step)
                pltpu.make_async_copy(w_in.at[0, rows], w.at[rows], recv_w.at[tree, step]).start()
                return carry

            lax.fori_loop(0, TREE_STEPS[tree], load, 0)

    foreign_cols = pl.ds(pl.multiple_of(((1 - y_hi) * 4 + x) * FEATS, FEATS), FEATS)
    own_cols = pl.ds(pl.multiple_of(tp * FEATS, FEATS), FEATS)
    wo_local = (
        pltpu.make_async_copy(wo_in.at[:, foreign_cols], wo.at[0, :, pl.ds(0, FEATS)], loc_wo.at[0]),
        pltpu.make_async_copy(wo_in.at[:, own_cols], wo.at[0, :, pl.ds(FEATS, FEATS)], loc_wo.at[1]),
    )
    for copy in wo_local:
        copy.start()

    eye = (
        lax.broadcasted_iota(jnp.int32, (128, 128), 0) == lax.broadcasted_iota(jnp.int32, (128, 128), 1)
    ).astype(F32)
    gain_row = gain[pl.ds(pl.multiple_of(tp * FEATS, FEATS), FEATS)].reshape(1, FEATS)
    for g in range(4):
        wide = hidden[pl.ds(g * 128, 128), :].astype(F32)
        xs[0, pl.ds(g * 128, 128), :] = (wide * gain_row).astype(BF16)

    pl.semaphore_wait(barrier, len(greeted))

    def piece(slot, p):
        return xs.at[slot, pl.ds(p * PIECE, PIECE)]

    def landed(block, p):
        return xl.at[block, pl.ds(p * PIECE, PIECE)]

    def send_piece(src, dst, sem, r_sem, to):
        send(src, dst, send_x.at[sem], r_sem, to).start()

    def wait_piece(slot, p):
        pltpu.make_async_copy(piece(slot, p), piece(slot, p), recv_x.at[slot, p]).wait()

    def wait_landed(block, p):
        pltpu.make_async_copy(landed(block, p), landed(block, p), recv_l.at[block, p]).wait()

    def to_final(src, slot, p, sem, to):
        send_piece(src, piece(slot, p), sem, recv_x.at[slot, p], to)

    def to_relay(src, block, p, sem, to):
        send_piece(src, landed(block, p), sem, recv_l.at[block, p], to)

    def cross(p):
        to_final(piece(0, p), 4, p, 2, opposite)
        to_relay(landed(3, p), 1, p, 2, opposite)

    @pl.when(relays_w)
    def _():
        for p in range(N_PIECES):
            to_relay(piece(0, p), 3, p, 2, sibling)

    @pl.when(relays_x)
    def _():
        for p in range(N_PIECES):
            to_final(piece(0, p), 2, p, 0, right)
            to_final(piece(0, p), 1, p, 1, left)
            wait_landed(3, p)
            if p % 2 == 0:
                to_relay(landed(3, p), 0, p, 0, right)
                to_final(landed(3, p), 1, p, 1, left_other)
            else:
                to_final(landed(3, p), 2, p, 0, right_other)
                to_relay(landed(3, p), 0, p, 1, left)
            if p in Y_FIRST:
                cross(p)

    def share_sums():
        sums[tp] = jnp.zeros((8, 128), F32)
        for g in range(4):
            wide = hidden[pl.ds(g * 128, 128), :].astype(F32)
            column = jnp.sum(wide * wide, axis=1, keepdims=True)
            sums[tp, pl.ds(g, 1), :] = jnp.sum(column * eye, axis=0, keepdims=True)
        for other in peers:
            send(sums.at[tp], sums.at[tp], send_s, recv_s.at[tp], other).start()


    def wo_block(quarter):
        return wo.at[pl.ds(1, 3), pl.ds(pl.multiple_of(lax.rem(z + quarter, 4) * 128, 128), 128), :]

    wo_targets = ((2, right_other, 1), (1, left_other, 3), (3, across_other, 2))

    def wo_sends(turn):
        rows = pl.ds(pl.multiple_of(lax.rem(z + 2 * turn, 4) * 128, 128), 128)
        for slot, to, shift in wo_targets:
            x_to = lax.rem(x + shift, 4)
            for part, y_part in ((0, 1 - y_hi), (1, y_hi)):
                cols = pl.ds(pl.multiple_of((y_part * 4 + x_to) * FEATS, FEATS), FEATS)
                send(
                    wo_in.at[rows, cols],
                    wo.at[slot, rows, pl.ds(part * FEATS, FEATS)],
                    send_wx.at[turn, slot - 1, part],
                    recv_wx.at[turn, slot - 1, part],
                    to,
                ).start()

    sends_tree = [
        [((MASKS[tree][dim] >> node) & 1) == 1 for dim in range(3)] for tree in range(3)
    ]

    def weight_tree(tree, step):
        rows = chunk(tree, step)
        pltpu.make_async_copy(w.at[rows], w.at[rows], recv_w.at[tree, step]).wait()
        for dim in range(3):
            if MASKS[tree][dim]:

                @pl.when(sends_tree[tree][dim])
                def _(dim=dim):
                    send(w.at[rows], w.at[rows], send_w.at[dim], recv_w.at[tree, step], dims[dim]).start()

        @pl.when(is_source)
        def _():
            turn = lax.rem(step, AHEAD)

            @pl.when(step >= AHEAD)
            def _():
                pltpu.make_async_copy(w.at[rows], w.at[rows], send_r.at[tree, turn]).wait()

            send(w.at[rows], w.at[rows], send_r.at[tree, turn], recv_w.at[tree, step], dims[tree]).start()

        send(w.at[rows], w.at[rows], send_sib, recv_w.at[tree, step], sibling).start()

    def wo_arrived(turn):
        rows = pl.ds(pl.multiple_of(lax.rem(z + 2 * turn, 4) * 128, 128), 128)
        for slot in range(3):
            for part in range(2):
                dst = wo.at[slot + 1, rows, pl.ds(part * FEATS, FEATS)]
                pltpu.make_async_copy(dst, dst, recv_wx.at[turn, slot, part]).wait()

    def wo_to_sibling(quarter):
        block = wo_block(quarter)
        send(block, block, send_ws.at[quarter], recv_ws.at[quarter], sibling).start()

    def wo_spread():
        wo_arrived(0)
        block = wo_block(0)
        for k, to in ((0, z_others[0]), (1, z_others[2])):
            send(block, block, send_wz.at[k], recv_wz.at[k], to).start()
        wo_to_sibling(0)

    def wo_pass(k):
        quarter = 3 - 2 * k
        block = wo_block(quarter)
        pltpu.make_async_copy(block, block, recv_wz.at[k]).wait()
        wo_to_sibling(quarter)

    def weight_steps():
        def slot_of(slot, carry):
            for tree in range(3):
                step = slot - LAG * ((DEPTHS[tree] >> (3 * node)) & 7)

                @pl.when(jnp.logical_and(step >= 0, step < TREE_STEPS[tree]))
                def _(tree=tree, step=step):
                    weight_tree(tree, step)

            return carry

        lax.fori_loop(0, N_SLOTS, slot_of, 0)

    def relay_ring(h, e):
        p = 2 * e
        wait_piece(4 * h + 2, p)
        to_final(piece(4 * h + 2, p), 4 * h + 3, p, 0, right)
        wait_landed(2 * h, p)
        to_final(landed(2 * h, p), 4 * h + 3, p, 0, right_other)
        to_final(landed(2 * h, p), 4 * h + 2, p, 3, sibling)
        p = 2 * e + 1
        wait_piece(4 * h + 1, p)
        to_final(piece(4 * h + 1, p), 4 * h + 3, p, 1, left)
        wait_landed(2 * h, p)
        to_final(landed(2 * h, p), 4 * h + 3, p, 1, left_other)
        to_final(landed(2 * h, p), 4 * h + 1, p, 3, sibling)

    def relay_opposite(p):
        wait_piece(4, p)
        to_final(piece(4, p), 6, p, 0, right)
        to_final(piece(4, p), 5, p, 1, left)
        wait_landed(1, p)
        if p % 2 == 0:
            to_relay(landed(1, p), 2, p, 0, right)
            to_final(landed(1, p), 5, p, 1, left_other)
        else:
            to_final(landed(1, p), 6, p, 0, right_other)
            to_relay(landed(1, p), 2, p, 1, left)
        to_final(landed(1, p), 4, p, 3, sibling)

    length = [lengths[0, k] for k in range(3)]
    begins = [length[0], length[0] + length[1], length[0] + length[1] + length[2]]

    def start_of(row):
        start = jnp.zeros_like(row)
        for begin in begins:
            start = jnp.where(row >= begin, begin, start)
        return start

    def fill_tables():
        cosine[...], sine[...] = rope_tables(start_of, ROWS)

    @pl.when(relays_w)
    def _():
        weight_steps()
        wo_spread()
        share_sums()
        fill_tables()

    @pl.when(relays_x)
    def _():
        share_sums()
        fill_tables()
        relay_ring(0, 0)
        relay_ring(0, 1)
        wo_sends(0)
        relay_opposite(0)
        relay_opposite(1)
        relay_ring(1, 0)
        for p in range(N_PIECES):
            if p not in Y_FIRST:
                cross(p)
        relay_opposite(2)
        relay_opposite(3)
        relay_ring(1, 1)
        wo_sends(1)

    @pl.when(relays_x)
    def _():
        for tree in range(3):

            def passed(step, carry, tree=tree):
                rows = chunk(tree, step)
                pltpu.make_async_copy(w.at[rows], w.at[rows], recv_w.at[tree, step]).wait()
                return carry

            lax.fori_loop(0, TREE_STEPS[tree], passed, 0)

    acc[...] = jnp.zeros_like(acc)

    def block_dot(slot, carry):
        turn = lax.rem(slot, 4)
        h = slot // 4

        for p in range(N_PIECES):
            relayed = (turn == 0) | ((turn == 2) & (p % 2 == 0)) | ((turn == 1) & (p % 2 == 1))
            seen = (slot == 0) | (relays_x & relayed)

            @pl.when(jnp.logical_not(seen))
            def _(p=p):
                wait_piece(slot, p)

        shift = jnp.where(turn == 2, 3, jnp.where(turn == 3, 2, turn))
        owner = lax.rem(y_hi + h, 2) * 4 + lax.rem(x + shift, 4)
        base = pl.multiple_of(owner * FEATS, FEATS)
        for n in range(3):
            cols = pl.ds(n * 256, 256)
            acc[:, cols] += jnp.dot(
                xs[slot], w[pl.ds(base, FEATS), cols], preferred_element_type=F32
            )
        return carry

    lax.fori_loop(0, 8, block_dot, 0)

    for k in range(1, N_TP):
        sender = lax.rem(tp + k, N_TP)
        pltpu.make_async_copy(sums.at[sender], sums.at[sender], recv_s.at[sender]).wait()
    total = sums[0]
    for t in range(1, N_TP):
        total = total + sums[t]
    factor = lax.rsqrt(total * (1.0 / D) + EPSILON)
    for g in range(4):
        inv[pl.ds(g * 128, 128), :] = jnp.sum(factor[g : g + 1, :] * eye, axis=1, keepdims=True) * jnp.ones(
            (1, 128), F32
        )

    def turned(value, rows):
        return value * cosine[rows, :] + pltpu.roll(value, HD // 2, axis=1) * sine[rows, :]

    def split(g, carry):
        rows = pl.ds(pl.multiple_of(g * 128, 128), 128)
        scale = inv[rows, :]
        for head in range(HEADS):
            qb[head, rows, :] = turned(acc[rows, pl.ds(head * HD, HD)] * scale, rows).astype(BF16)
        kb[rows, :] = turned(acc[rows, pl.ds(ATT_COLS, HD)] * scale, rows).astype(BF16)
        vb[rows, :] = (acc[rows, pl.ds(ATT_COLS + HD, HD)] * scale).astype(BF16)
        return carry

    lax.fori_loop(0, 4, split, 0)

    def att_rows(slot, q):
        return att.at[slot, pl.ds(q * TQ, TQ)]

    def att_half(slot, q, half):
        return att.at[slot, pl.ds(q * TQ + half * (TQ // 2), TQ // 2)]

    for q in range(N_Q):
        low = max(0, q * TQ - LONGEST)
        high = (q + 1) * TQ
        row = lax.broadcasted_iota(jnp.int32, (TQ, high - low), 0) + q * TQ
        key = lax.broadcasted_iota(jnp.int32, (TQ, high - low), 1) + low
        allowed = (key <= row) & (key >= start_of(row))
        for head in range(HEADS):
            scores = lax.dot_general(
                qb[head, pl.ds(q * TQ, TQ), :],
                kb[pl.ds(low, high - low), :],
                (((1,), (1,)), ((), ())),
                preferred_element_type=F32,
            ) * (1.0 / math.sqrt(HD))
            scores = jnp.where(allowed, scores, -1e30)
            largest = jnp.max(scores, axis=1, keepdims=True)
            weights = jnp.exp(jnp.where(allowed, scores - largest, -1e30))
            denominator = jnp.sum(weights, axis=1, keepdims=True)
            mixed = jnp.dot(weights.astype(BF16), vb[pl.ds(low, high - low), :], preferred_element_type=F32)
            att[0, pl.ds(q * TQ, TQ), pl.ds(head * HD, HD)] = (mixed / denominator).astype(BF16)
        send(att_rows(0, q), att_rows(2, q), send_a.at[0], recv_a.at[1, q], right).start()
        send(att_rows(0, q), att_rows(1, q), send_a.at[1], recv_a.at[0, q], left).start()

        @pl.when(relays_w)
        def _(q=q):
            if q == 3:
                wo_pass(0)
                wo_pass(1)
                wo_arrived(1)
                wo_to_sibling(2)

    for copy in wo_local:
        copy.wait()

    @pl.when(relays_x)
    def _():
        for quarter in range(4):
            block = wo_block(quarter)
            pltpu.make_async_copy(block, block, recv_ws.at[quarter]).wait()

    def relay_att(q):
        pltpu.make_async_copy(att_rows(2, q), att_rows(2, q), recv_a.at[1, q]).wait()
        send(att_half(2, q, 0), att_half(3, q, 0), send_a.at[0], recv_a.at[2, q], right).start()
        pltpu.make_async_copy(att_rows(1, q), att_rows(1, q), recv_a.at[0, q]).wait()
        send(att_half(1, q, 1), att_half(3, q, 1), send_a.at[1], recv_a.at[3, q], left).start()

    def tile(q, cols):
        total = jnp.dot(att[0, pl.ds(q * TQ, TQ), :], wo[0, :, cols], preferred_element_type=F32)
        for slot in range(1, 4):
            total += jnp.dot(att[slot, pl.ds(q * TQ, TQ), :], wo[slot, :, cols], preferred_element_type=F32)
        return total

    def foreign_part(q):
        for half in range(2):
            pltpu.make_async_copy(att_half(3, q, half), att_half(3, q, half), recv_a.at[2 + half, q]).wait()

        def foreign(n, carry):
            cols = pl.ds(pl.multiple_of(n * 256, 256), 256)
            pf[pl.ds(q * TQ, TQ), cols] = tile(q, cols).astype(BF16)
            return carry

        lax.fori_loop(0, 4, foreign, 0)
        rows = pl.ds(q * TQ, TQ)
        send(pf.at[rows], rb.at[rows], send_y, recv_y.at[q], opposite).start()

    def own_part(q):
        def mine(n, carry):
            cols = pl.ds(pl.multiple_of(n * 256, 256), 256)
            own[pl.ds(q * TQ, TQ), cols] = tile(q, pl.ds(pl.multiple_of(FEATS + n * 256, 256), 256))
            return carry

        lax.fori_loop(0, 4, mine, 0)

    relay_att(0)
    for q in range(N_Q):
        if q + 1 < N_Q:
            relay_att(q + 1)
        foreign_part(q)
    for q in range(N_Q):
        own_part(q)
    for q in range(N_Q):
        rows = pl.ds(q * TQ, TQ)
        pltpu.make_async_copy(rb.at[rows], rb.at[rows], recv_y.at[q]).wait()
        out[rows, :] = (own[rows, :] + rb[rows, :].astype(F32)).astype(BF16)

    def sent(ref, sem):
        pltpu.make_async_copy(ref, ref, sem).wait()

    @pl.when(relays_w)
    def _():
        for tree in range(3):
            for dim in range(3):
                if MASKS[tree][dim]:

                    @pl.when(sends_tree[tree][dim])
                    def _(tree=tree, dim=dim):
                        sent(w.at[pl.ds(0, TREE_STEPS[tree] * CHUNK)], send_w.at[dim])

        @pl.when(is_source)
        def _():
            for tree in range(3):
                for turn in range(AHEAD):
                    sent(w.at[pl.ds(0, CHUNK)], send_r.at[tree, turn])

        sent(w, send_sib)
        sent(xs.at[0], send_x.at[2])
        for k in range(2):
            sent(wo_block(0), send_wz.at[k])
        for quarter in range(4):
            sent(wo_block(0), send_ws.at[quarter])

    @pl.when(relays_x)
    def _():
        for side in range(2):
            sent(xs.at[pl.ds(0, 6)], send_x.at[side])
        sent(xs.at[pl.ds(0, 2)], send_x.at[2])
        sent(xs.at[pl.ds(0, 3)], send_x.at[3])
        for turn in range(2):
            for slot in range(3):
                for part in range(2):
                    sent(wo.at[0, pl.ds(0, 128), pl.ds(0, FEATS)], send_wx.at[turn, slot, part])

    sent(sums.at[pl.ds(0, 7)], send_s)
    for side in range(2):
        sent(att.at[0], send_a.at[side])
        sent(att.at[0, pl.ds(0, ROWS // 2)], send_a.at[side])
    sent(pf, send_y)


def local(hidden_rows, lengths, attn_gain, w_joined, w_out):
    dma = pltpu.SemaphoreType.DMA
    vmem = pl.BlockSpec(memory_space=pltpu.VMEM)
    anywhere = pl.BlockSpec(memory_space=pl.ANY)
    return pl.pallas_call(
        body,
        out_shape=jax.ShapeDtypeStruct((ROWS, FEATS), BF16),
        in_specs=[vmem, pl.BlockSpec(memory_space=pltpu.SMEM), vmem, anywhere, anywhere],
        out_specs=vmem,
        scratch_shapes=[
            pltpu.VMEM((D, COLS), BF16),
            pltpu.VMEM((8, ROWS, FEATS), BF16),
            pltpu.VMEM((4, ROWS, FEATS), BF16),
            pltpu.VMEM((4, ATT_COLS, 2 * FEATS), BF16),
            pltpu.VMEM((ROWS, COLS), F32),
            pltpu.VMEM((4, ROWS, ATT_COLS), BF16),
            pltpu.VMEM((ROWS, FEATS), BF16),
            pltpu.VMEM((ROWS, FEATS), BF16),
            pltpu.VMEM((ROWS, FEATS), F32),
            pltpu.VMEM((N_TP, 8, 128), F32),
            pltpu.VMEM((ROWS, 128), F32),
            pltpu.VMEM((ROWS, HD), F32),
            pltpu.VMEM((ROWS, HD), F32),
            pltpu.VMEM((HEADS, ROWS, HD), BF16),
            pltpu.VMEM((ROWS, HD), BF16),
            pltpu.VMEM((ROWS, HD), BF16),
            dma((3, max(TREE_STEPS))),
            dma((3,)),
            dma((3, AHEAD)),
            dma,
            dma((8, N_PIECES)),
            dma((4, N_PIECES)),
            dma((4,)),
            dma((N_TP,)),
            dma,
            dma((2, 3, 2)),
            dma((2, 3, 2)),
            dma((2,)),
            dma((2,)),
            dma((4,)),
            dma((4,)),
            dma((2,)),
            dma((4, N_Q)),
            dma((2,)),
            dma((N_Q,)),
            dma,
        ],
        compiler_params=pltpu.CompilerParams(
            collective_id=0, has_side_effects=True, vmem_limit_bytes=56 * 1024 * 1024
        ),
    )(hidden_rows, lengths, attn_gain, w_joined, w_out)


def solution(mesh):
    return jax.shard_map(
        local,
        mesh=mesh,
        in_specs=(P("inst", "tp"), P("inst", None), P(), P("inst", None, "tp"), P("tp", None)),
        out_specs=P("inst", "tp"),
        check_vma=False,
    )
```
